32 devices in a mesh: grp: 8 (over z, x), sub: 4 (over y, core).
Axes of the slice: x: 2, y: 2, z: 4, core: 2. Of those that a mesh axis runs over, the one named last changes fastest.
Arguments:
- load: float32 [8, 4, 15, 384], P('grp', 'sub'), may hold values from -6 to 6
- couple: bfloat16 [8, 4, 4, 15, 15, 384], P('grp', 'sub'), may hold values from -1 to 6
- face_link: int32 [8, 4, 3, 384], P('grp', 'sub'), may hold values from 0 to 383, as said below
- face_count: int32 [8, 4], P('grp', 'sub'), may hold values from 192 to 384, as said below
- slot_face: int32 [8, 4, 4, 32], P('grp', 'sub'), may hold values from 0 to 383, as said below
- pair_count: int32 [8, 4, 4], P('grp', 'sub'), may hold values from 0 to 32, as said below
- basis: float32 [8, 4, 64, 15, 384], P('grp', 'sub'), may hold values from -0.0390625 to 0.0390625
- coarse_inverse: float32 [8, 4, 64, 64], P('grp', 'sub'), may hold values from -0.25 to 1.65
- coarse_block: float32 [8, 4, 6, 64, 64], P('grp', 'sub'), may hold values from -0.15625 to 0.15625
- coarse_link: int32 [8, 4, 6], P('grp', 'sub'), may hold values from 0 to 31, as said below
Outputs:
- trace_field: float32 [8, 4, 15, 384], P('grp', 'sub')
- robin_data: float32 [8, 4, 15, 384], P('grp', 'sub')
- coarse_coef: float32 [8, 4, 64], P('grp', 'sub')
The draws below stay inside these ranges and needn't reach their ends.
Inputs may be any that keep to these rules, and one draw needn't show every extreme that they name: Subdomain (g, i) has live face blocks 0 to face_count[g, i] - 1; the rest are padding. Some subdomain has all 384 live. pair_count[g, i, j] equals pair_count[g, j, i], is 0 for j = i and otherwise 1 or more, a quarter of 32 or more, rounded down; every subdomain has exactly one peer with 32, and all its other peers have half of 32 or fewer. `slot_face`: for c < pair_count[g, i, j], slot c toward j names a live face block of i that i shares with j, the same face that slot c of j toward i names on j's side; these faces are distinct within a subdomain. Other slots name any face block. `face_link`: linked face blocks are live and differ from the face block itself. `coarse_link`: the 6 coarse neighbours of subdomain (g, i) are distinct, differ from it, and lie in groups g - 1, g or g + 1.
All inputs are finite; a program needn't handle non-finite values.
Results may differ from the reference program's by a relative error of at most 0.0015.
Values sent between devices are 32-bit elements; how exact they have to be, the bound alone decides.
A program may use at most 64 MiB of HBM per device.

```python
import jax
import jax.numpy as jnp
from jax import lax

TRACE = 15
FB = 384
CAP = 32
LINKS = 3
CVEC = 64
KC = 6
ITERS = 3
SWEEPS = 2
CSWEEPS = 2
GROUPS = 8
PEERS = 4


def face_counts(key):
    count_key = jax.random.fold_in(key, 11)
    interface_most = CAP + (PEERS - 2) * (CAP // 2)
    lower = max(interface_most, FB // 2)
    counts = jax.random.randint(count_key, (GROUPS * PEERS,), lower, FB + 1)
    chosen = jax.random.randint(jax.random.fold_in(count_key, 1), (), 0, GROUPS * PEERS)
    counts = jnp.where(jnp.arange(GROUPS * PEERS) == chosen, FB, counts)
    return counts.reshape(GROUPS, PEERS).astype(jnp.int32)


def shuffle(group_key):
    return jax.random.permutation(group_key, PEERS)


def pair_counts(key):
    light_low = max(1, CAP // 4)
    light_count = jax.random.randint(jax.random.fold_in(key, 23), (GROUPS, PEERS, PEERS), light_low, CAP // 2 + 1)
    row_index = jnp.arange(PEERS)[:, None]
    col_index = jnp.arange(PEERS)[None, :]
    symmetric = jnp.where(row_index < col_index, light_count, jnp.swapaxes(light_count, 1, 2))
    group_keys = jax.random.split(jax.random.fold_in(key, 29), GROUPS)
    orders = jax.vmap(shuffle)(group_keys).astype(jnp.int32)
    position = jnp.argsort(orders, axis=1).astype(jnp.int32)
    partner = jnp.take_along_axis(orders, jnp.bitwise_xor(position, 1), axis=1)
    heavy_pair = partner[:, :, None] == col_index[None]
    result = jnp.where(heavy_pair, CAP, symmetric)
    result = jnp.where(row_index == col_index, 0, result)
    return result.astype(jnp.int32)


def draw_face_count(key, part):
    return face_counts(key)


def draw_pair_count(key, part):
    return pair_counts(key)


def draw_slot_face(key, part):
    counts = face_counts(key)
    pairs = pair_counts(key)
    face_ids = jnp.arange(FB, dtype=jnp.int32)
    scores = jax.random.randint(jax.random.fold_in(key, 37), (GROUPS, PEERS, FB), 0, 2 ** 19) * FB + face_ids
    active = face_ids[None, None, :] < counts[:, :, None]
    scores = jnp.where(active, scores, 2 ** 30 + face_ids)
    ranking = jnp.argsort(scores, axis=-1).astype(jnp.int32)
    offsets = jnp.cumsum(pairs, axis=-1) - pairs
    position = offsets[..., None] + jnp.arange(CAP, dtype=jnp.int32)
    position = jnp.minimum(position, FB - 1).reshape(GROUPS, PEERS, PEERS * CAP)
    chosen_faces = jnp.take_along_axis(ranking, position, axis=-1)
    return chosen_faces.reshape(GROUPS, PEERS, PEERS, CAP).astype(jnp.int32)


def draw_face_link(key, part):
    counts = face_counts(key)
    random_ints = jax.random.randint(jax.random.fold_in(key, 41), (GROUPS, PEERS, LINKS, FB), 0, 2 ** 20)
    face_ids = jnp.arange(FB, dtype=jnp.int32)
    live_count = counts[:, :, None, None]
    face_pick = (face_ids + 1 + random_ints % (live_count - 1)) % live_count
    return face_pick.astype(jnp.int32)


def draw_coarse_link(key, part):
    candidate = jnp.arange(3 * PEERS, dtype=jnp.int32)
    group_ids = jnp.arange(GROUPS, dtype=jnp.int32)[:, None, None]
    sub_ids = jnp.arange(PEERS, dtype=jnp.int32)[None, :, None]
    near_group = group_ids - 1 + candidate // PEERS
    near_sub = candidate % PEERS
    invalid = (near_group < 0) | (near_group >= GROUPS) | (near_group == group_ids) & (near_sub == sub_ids)
    scores = jax.random.randint(jax.random.fold_in(key, 53), (GROUPS, PEERS, 3 * PEERS), 0, 2 ** 20) * (3 * PEERS) + candidate
    scores = jnp.where(invalid, 2 ** 30 + candidate, scores)
    picked = jnp.argsort(scores, axis=-1)[..., :KC].astype(jnp.int32)
    global_ids = (group_ids - 1 + picked // PEERS) * PEERS + picked % PEERS
    return global_ids.astype(jnp.int32)


def draw_couple(key, part):
    full_shape = (GROUPS, PEERS, LINKS + 1, TRACE, TRACE, FB)
    noise_part = jnp.clip(0.2 * jax.random.normal(jax.random.fold_in(key, 61), full_shape, jnp.float32), -1.0, 1.0)
    diagonal = jax.random.uniform(jax.random.fold_in(key, 67), (GROUPS, PEERS, 1, TRACE, 1, FB), jnp.float32, 3.0, 5.0)
    identity = jnp.eye(TRACE, dtype=jnp.float32)[:, :, None]
    first_block = (jnp.arange(LINKS + 1) == 0).astype(jnp.float32)[:, None, None, None]
    return (noise_part + first_block * identity * diagonal).astype(jnp.bfloat16)


def draw_coarse_inverse(key, part):
    full_shape = (GROUPS, PEERS, CVEC, CVEC)
    noise_part = jnp.clip(0.04 * jax.random.normal(jax.random.fold_in(key, 71), full_shape, jnp.float32), -0.25, 0.25)
    diagonal = jax.random.uniform(jax.random.fold_in(key, 73), (GROUPS, PEERS, CVEC, 1), jnp.float32, 0.6, 1.4)
    identity = jnp.eye(CVEC, dtype=jnp.float32)
    return (noise_part + identity * diagonal).astype(jnp.float32)


def shard_levels(stream_key, shape, shards, low, top_value):
    gain, own = 1.0, jax.random.fold_in(stream_key, 6)
    for axis_at, parts in shards:
        draws = jnp.exp(jax.random.uniform(jax.random.fold_in(own, axis_at), (parts,), jnp.float32, low / len(shards), top_value / len(shards)))
        gain = gain * jnp.repeat(draws, shape[axis_at] // parts).reshape([-1 if axis == axis_at else 1 for axis in range(len(shape))])
    return gain


def bell_draw(own_key, dims, width, most, pieces=(), held_as=jnp.bfloat16):
    entries = width * jax.random.normal(own_key, dims, jnp.float32)
    if pieces:
        entries = entries * shard_levels(own_key, dims, pieces, -0.22, 0.18)
    return jnp.clip(entries, -most, most).astype(held_as)


def setup_inputs(seed: int = 0) -> dict:
    streams_of = jax.random.split(jax.random.key(seed), 11)
    return {
        "load": bell_draw(streams_of[0], (GROUPS, PEERS, TRACE, FB), 1.0, 6.0, ((0, 8), (1, 4)), jnp.float32),
        "couple": draw_couple(jax.random.fold_in(streams_of[10], 71), 0),
        "face_link": draw_face_link(jax.random.fold_in(streams_of[10], 71), 0),
        "face_count": draw_face_count(jax.random.fold_in(streams_of[10], 71), 0),
        "slot_face": draw_slot_face(jax.random.fold_in(streams_of[10], 71), 0),
        "pair_count": draw_pair_count(jax.random.fold_in(streams_of[10], 71), 0),
        "basis": bell_draw(streams_of[6], (GROUPS, PEERS, CVEC, TRACE, FB), (4 * TRACE * FB) ** -0.5, 0.0390625, ((0, 8), (1, 4)), jnp.float32),
        "coarse_inverse": draw_coarse_inverse(jax.random.fold_in(streams_of[10], 71), 0),
        "coarse_block": bell_draw(streams_of[8], (GROUPS, PEERS, KC, CVEC, CVEC), (4 * KC * CVEC) ** -0.5, 0.15625, ((0, 8), (1, 4)), jnp.float32),
        "coarse_link": draw_coarse_link(jax.random.fold_in(streams_of[10], 71), 0),
    }


robin_weight = 1.0
omega_step = 0.2
highest = lax.Precision.HIGHEST


def couple_apply(couple, face_links, trace_rows, live_mask, interface):
    linked = jnp.moveaxis(trace_rows[:, face_links], 1, 0)
    stacked = jnp.concatenate([trace_rows[None], linked], axis=0)
    product = jnp.sum(couple * stacked[:, None, :, :], axis=(0, 2))
    return live_mask * (product + robin_weight * interface * trace_rows)


def masks_for(own_count, own_slots, own_pairs):
    live_mask = (jnp.arange(FB) < own_count).astype(jnp.float32)
    valid_slots = jnp.arange(CAP)[None, :] < own_pairs[:, None]
    counted = jnp.zeros((FB,), jnp.float32).at[own_slots].add(valid_slots.astype(jnp.float32))
    return live_mask, jnp.minimum(counted, 1.0), valid_slots


def local_phase(load_rows, couple, face_links, live_mask, interface, basis_rows, trace_field, robin_data):
    for sweep_index in range(SWEEPS):
        residual = live_mask * (load_rows + robin_data) - couple_apply(couple, face_links, trace_field, live_mask, interface)
        trace_field = trace_field + omega_step * residual
    residual = live_mask * (load_rows + robin_data) - couple_apply(couple, face_links, trace_field, live_mask, interface)
    restricted = jnp.dot(basis_rows.reshape(basis_rows.shape[0], -1), residual.reshape(-1), precision=highest)
    return trace_field, restricted


def run_groups(operands):
    return jax.vmap(local_phase)(*operands)


def take_slots(trace_rows, slot_rows):
    return trace_rows[:, slot_rows]


def add_slots(arrivals, slot_rows):
    return jnp.zeros((TRACE, FB), jnp.float32).at[:, slot_rows].add(arrivals)


def reference(load, couple, face_link, face_count, slot_face, pair_count, basis, coarse_inverse, coarse_block, coarse_link):
    live_mask, interface, valid_slots = jax.vmap(jax.vmap(masks_for))(face_count, slot_face, pair_count)
    trace_field = jnp.zeros(load.shape, jnp.float32)
    robin_data = jnp.zeros(load.shape, jnp.float32)
    coefficients = jnp.zeros((GROUPS, PEERS, CVEC), jnp.float32)
    for outer_step in range(ITERS):
        trace_field, restricted = lax.map(run_groups, (load, couple, face_link, live_mask, interface, basis, trace_field, robin_data))
        coarse_start = jnp.einsum("gpvw,gpw->gpv", coarse_inverse, restricted, precision=highest)
        coefficients = coarse_start
        for inner_step in range(CSWEEPS):
            flattened = coefficients.reshape(-1, CVEC)
            gathered = flattened[coarse_link]
            coupled = jnp.einsum("gpkvw,gpkw->gpv", coarse_block, gathered, precision=highest)
            coefficients = coarse_start - jnp.einsum("gpvw,gpw->gpv", coarse_inverse, coupled, precision=highest)
        correction = jnp.einsum("gpv,gpvaf->gpaf", coefficients, basis, precision=highest)
        trace_field = trace_field + live_mask[:, :, None, :] * correction
        outgoing = 2.0 * robin_weight * trace_field - robin_data
        sent = jax.vmap(jax.vmap(take_slots))(outgoing, slot_face)
        received = jnp.transpose(sent, (0, 3, 2, 1, 4))
        received = jnp.where(valid_slots[:, :, None, :, :], received, 0.0)
        robin_data = jax.vmap(jax.vmap(add_slots))(received, slot_face)
    return trace_field, robin_data, coefficients
```

```python
import functools

import jax
import jax.numpy as jnp
from jax import lax
from jax.experimental import pallas as pl
from jax.experimental.pallas import tpu as pltpu
from jax.sharding import PartitionSpec as P

ITERS = 3
SWEEPS = 2
CSWEEPS = 2
LANES = 128

robin_weight = 1.0
omega_step = 0.2
highest = lax.Precision.HIGHEST
MESH = pl.DeviceIdType.MESH


def pick_lanes(field, index):
    rows = field.shape[0]
    parts = []
    for d in range(index.shape[1] // LANES):
        wanted = jnp.broadcast_to(index[:, d * LANES : (d + 1) * LANES], (rows, LANES))
        within = lax.rem(wanted, LANES)
        chunk = lax.div(wanted, LANES)
        out = None
        for s in range(field.shape[1] // LANES):
            got = jnp.take_along_axis(
                field[:, s * LANES : (s + 1) * LANES], within, axis=1, mode="promise_in_bounds"
            )
            out = got if out is None else jnp.where(chunk == s, got, out)
        parts.append(out)
    return jnp.concatenate(parts, axis=1) if len(parts) > 1 else parts[0]


def iota(shape, dim):
    return lax.broadcasted_iota(jnp.int32, shape, dim)


def kernel(
    groups,
    peers,
    load_ref,
    couple_ref,
    link_ref,
    count_ref,
    slot_ref,
    pair_ref,
    basis_ref,
    inverse_ref,
    block_ref,
    coarse_link_ref,
    trace_out,
    robin_out,
    coef_out,
    load_s,
    trace_s,
    robin_s,
    bx_s,
    couple_s,
    moved_s,
    kept_s,
    table_s,
    folded_s,
    slots_s,
    back_s,
    interface_s,
    coarse_send,
    coarse_recv,
    robin_send,
    robin_recv,
    coarse_send_sem,
    coarse_recv_sem,
    robin_send_sem,
    robin_recv_sem,
):
    g, me = lax.axis_index("grp"), lax.axis_index("sub")
    trace_dim, faces = load_ref.shape[1], load_ref.shape[-1]
    rows = load_s.shape[0]
    cvec = inverse_ref.shape[-1]
    links = link_ref.shape[1]
    kc = coarse_link_ref.shape[-1]
    cap = slot_ref.shape[-1]
    slot_lanes = peers * cap

    def per_group(act):
        @pl.when(g > 0)
        def _():
            act(-1)

        @pl.when(g < groups - 1)
        def _():
            act(1)

        act(0)

    def targets(d):
        first = 1 if d == 0 else 0
        return [(g + d, lax.rem(me + off, peers)) for off in range(first, peers)]

    barrier = pltpu.get_barrier_semaphore()

    def greet(d):
        for device in targets(d):
            pl.semaphore_signal(barrier, inc=1, device_id=device, device_id_type=MESH)

    per_group(greet)

    live = (iota((1, faces), 1) < count_ref[0, 0]).astype(jnp.float32)
    load_s[...] = jnp.zeros_like(load_s)
    for a in range(trace_dim):
        load_s[a : a + 1, :] = load_ref[0, a] * live
    bx_s[...] = jnp.zeros_like(bx_s)
    moved_s[...] = jnp.zeros_like(moved_s)

    def unpack(a, carry):
        for s in range(faces // LANES):
            for k in range(links + 1):
                couple_s[s, a, (k + 1) * rows - 8 : (k + 1) * rows, :] = jnp.zeros((8, LANES), jnp.float32)
        for b in range(trace_dim):
            blocks = couple_ref[0, 0, a, b].astype(jnp.float32)
            for s in range(faces // LANES):
                couple_s[s, a, pl.ds(b, links + 1, stride=rows), :] = blocks[:, s * LANES : (s + 1) * LANES]
        return carry

    lax.fori_loop(0, trace_dim, unpack, 0)
    for k in range(kc):
        folded_s[k] = jnp.dot(
            inverse_ref[0, 0],
            block_ref[0, 0, k],
            precision=highest,
            preferred_element_type=jnp.float32,
        )
    coarse_send[...] = jnp.zeros_like(coarse_send)
    slots_s[...] = jnp.zeros_like(slots_s)
    back = jnp.zeros((1, faces), jnp.float32)
    hits = jnp.zeros((1, faces), jnp.float32)
    eye_slots = iota((cap, cap), 0) == iota((cap, cap), 1)
    for j in range(peers):
        slot_row = slot_ref[0, 0, j : j + 1, :]
        slots_s[:, j * cap : (j + 1) * cap] = slot_row
        as_float = jnp.broadcast_to(slot_row.astype(jnp.float32), (cap, cap))
        column = jnp.sum(jnp.where(eye_slots, as_float, 0.0), axis=1, keepdims=True)
        face_ids = iota((cap, faces), 1).astype(jnp.float32)
        place = iota((cap, faces), 0)
        hit = (column == face_ids) & (place < pair_ref[0, 0, j])
        hits = hits + jnp.sum(jnp.where(hit, 1.0, 0.0), axis=0, keepdims=True)
        back = back + jnp.sum(
            jnp.where(hit, (place + j * cap).astype(jnp.float32), 0.0), axis=0, keepdims=True
        )
    interface_s[...] = jnp.minimum(hits, 1.0)
    back_s[...] = back.astype(jnp.int32)
    robin_s[...] = jnp.zeros_like(robin_s)
    trace_s[...] = omega_step * load_s[...]
    eye = iota((cvec, cvec), 0) == iota((cvec, cvec), 1)

    count = (peers - 1) + jnp.where(g > 0, peers, 0) + jnp.where(g < groups - 1, peers, 0)
    pl.semaphore_wait(barrier, count)

    def apply(x):
        stacked = [x] + [
            pick_lanes(x, link_ref[0, k]) for k in range(links)
        ]
        for s in range(faces // LANES):
            lanes = slice(s * LANES, (s + 1) * LANES)
            for a in range(trace_dim):
                total = couple_s[s, a, 0:rows, :] * stacked[0][:, lanes]
                for k in range(1, links + 1):
                    total = total + couple_s[s, a, k * rows : (k + 1) * rows, :] * stacked[k][:, lanes]
                bx_s[a : a + 1, lanes] = jnp.sum(total, axis=0, keepdims=True)
        return live * (bx_s[...] + robin_weight * interface_s[...] * x)

    def right_side():
        return load_s[...] + live * robin_s[...]

    def sweep(x, bx):
        return x + omega_step * (right_side() - bx)

    def as_row(column):
        return jnp.sum(jnp.where(eye, column, 0.0), axis=0, keepdims=True)

    def send_row(t, r, row):
        coarse_send[t, r, :, 0:cvec] = row

        def push(d):
            for device in targets(d):
                pltpu.make_async_remote_copy(
                    src_ref=coarse_send.at[t, r],
                    dst_ref=coarse_recv.at[t, r, (1 - d) * peers + me],
                    send_sem=coarse_send_sem.at[t, r, 1 + d],
                    recv_sem=coarse_recv_sem.at[t, r, 1 - d],
                    device_id=device,
                    device_id_type=MESH,
                ).start()

        per_group(push)

    def wait_rows(t, r, sems):
        def wait(d):
            n = peers - 1 if d == 0 else peers
            part = coarse_recv.at[t, r, pl.ds((1 + d) * peers, n)]
            pltpu.make_async_copy(part, part, sems.at[t, r, 1 + d]).wait()

        per_group(wait)

    def coupled(t, r):
        table_s[...] = coarse_recv[t, r]
        total = None
        for k in range(kc):
            position = coarse_link_ref[0, 0, k] - (g - 1) * peers
            position = jnp.minimum(jnp.maximum(position, 0), 3 * peers - 1)
            term = folded_s[k] * table_s[position][:, 0:cvec]
            total = term if total is None else total + term
        return jnp.sum(total, axis=1, keepdims=True)

    def robin_copy(t, off):
        to = lax.rem(me + off, peers)
        chunk = lax.div(to * cap, LANES)
        return pltpu.make_async_remote_copy(
            src_ref=robin_send.at[t, chunk],
            dst_ref=robin_recv.at[t, off - 1],
            send_sem=robin_send_sem.at[t, off - 1],
            recv_sem=robin_recv_sem.at[t, off - 1],
            device_id=(g, to),
            device_id_type=MESH,
        )

    def iteration(t, carry):
        x = trace_s[...]
        for _ in range(SWEEPS - 1):
            x = sweep(x, apply(x))
        residual = right_side() - apply(x)
        trace_s[...] = x

        part = jnp.zeros((cvec, LANES), jnp.float32)
        for a in range(trace_dim):
            product = basis_ref[0, 0, a] * residual[a : a + 1, :]
            for s in range(faces // LANES):
                part = part + product[:, s * LANES : (s + 1) * LANES]
        restricted = jnp.sum(part, axis=1, keepdims=True)
        start = jnp.sum(inverse_ref[0, 0] * as_row(restricted), axis=1, keepdims=True)
        coef = start
        for r in range(CSWEEPS):
            send_row(t, r, as_row(coef))
            wait_rows(t, r, coarse_recv_sem)
            coef = start - coupled(t, r)
        coef_out[0] = as_row(coef)
        wide = jnp.broadcast_to(coef, (cvec, faces))
        for a in range(trace_dim):
            moved_s[a : a + 1, :] = jnp.sum(basis_ref[0, 0, a] * wide, axis=0, keepdims=True)
        x = trace_s[...] + live * moved_s[...]
        kept_s[...] = x
        outgoing = 2.0 * robin_weight * x - robin_s[...]
        sent = pick_lanes(outgoing, slots_s[...])
        for s in range(slots_s.shape[1] // LANES):
            robin_send[t, s] = sent[:, s * LANES : (s + 1) * LANES]
        for off in range(1, peers):
            robin_copy(t, off).start()
        bx = apply(x)
        wanted = back_s[...]
        inside = lax.rem(wanted, cap)
        base = lax.rem(me * cap, LANES)
        owner = lax.div(wanted, cap)
        fresh = jnp.zeros((rows, faces), jnp.float32)
        for off in range(1, peers):
            robin_copy(t, off).wait_recv()
            source = lax.rem(me + peers - off, peers)
            got = pick_lanes(robin_recv[t, off - 1], inside + base)
            fresh = jnp.where((owner == source) & (interface_s[...] > 0.0), got, fresh)
        robin_s[...] = fresh
        trace_s[...] = sweep(x, bx)
        for r in range(CSWEEPS):
            wait_rows(t, r, coarse_send_sem)
        for off in range(1, peers):
            robin_copy(t, off).wait_send()
        return carry

    lax.fori_loop(0, ITERS, iteration, 0)
    for a in range(trace_dim):
        trace_out[0, a] = kept_s[a : a + 1, :]
        robin_out[0, a] = robin_s[a : a + 1, :]


def solution(mesh):
    groups, peers = mesh.shape["grp"], mesh.shape["sub"]

    def body(
        load,
        couple,
        face_link,
        face_count,
        slot_face,
        pair_count,
        basis,
        coarse_inverse,
        coarse_block,
        coarse_link,
    ):
        trace_dim, faces = load.shape[-2:]
        rows = -(-trace_dim // 8) * 8
        links = face_link.shape[-2]
        cvec = basis.shape[2]
        kc = coarse_link.shape[-1]
        cap = slot_face.shape[-1]
        chunks = -(-peers * cap // LANES)
        vmem, smem = pltpu.VMEM, pltpu.SMEM
        f32 = jnp.float32
        spec = lambda space: pl.BlockSpec(memory_space=space)
        trace_field, robin_data, coefficients = pl.pallas_call(
            functools.partial(kernel, groups, peers),
            out_shape=(
                jax.ShapeDtypeStruct((1, trace_dim, 1, faces), f32),
                jax.ShapeDtypeStruct((1, trace_dim, 1, faces), f32),
                jax.ShapeDtypeStruct((1, 1, cvec), f32),
            ),
            in_specs=[
                spec(vmem),
                spec(vmem),
                spec(vmem),
                spec(smem),
                spec(vmem),
                spec(smem),
                spec(vmem),
                spec(vmem),
                spec(vmem),
                spec(smem),
            ],
            out_specs=(spec(vmem), spec(vmem), spec(vmem)),
            scratch_shapes=[
                vmem((rows, faces), f32),
                vmem((rows, faces), f32),
                vmem((rows, faces), f32),
                vmem((rows, faces), f32),
                vmem((faces // LANES, trace_dim, (links + 1) * rows, LANES), f32),
                vmem((rows, faces), f32),
                vmem((rows, faces), f32),
                vmem((3 * peers, 1, LANES), f32),
                vmem((kc, cvec, cvec), f32),
                vmem((1, chunks * LANES), jnp.int32),
                vmem((1, faces), jnp.int32),
                vmem((1, faces), f32),
                vmem((ITERS, CSWEEPS, 1, LANES), f32),
                vmem((ITERS, CSWEEPS, 3 * peers, 1, LANES), f32),
                vmem((ITERS, chunks, rows, LANES), f32),
                vmem((ITERS, peers - 1, rows, LANES), f32),
                pltpu.SemaphoreType.DMA((ITERS, CSWEEPS, 3)),
                pltpu.SemaphoreType.DMA((ITERS, CSWEEPS, 3)),
                pltpu.SemaphoreType.DMA((ITERS, peers - 1)),
                pltpu.SemaphoreType.DMA((ITERS, peers - 1)),
            ],
            compiler_params=pltpu.CompilerParams(
                collective_id=0, has_side_effects=True, vmem_limit_bytes=32 * 1024 * 1024
            ),
        )(
            jnp.swapaxes(load, 1, 2),
            jnp.transpose(couple, (0, 1, 3, 4, 2, 5)),
            jnp.swapaxes(face_link, 1, 2),
            face_count,
            slot_face,
            pair_count,
            jnp.swapaxes(basis, 2, 3),
            coarse_inverse,
            coarse_block,
            coarse_link,
        )
        return jnp.swapaxes(trace_field, 1, 2), jnp.swapaxes(robin_data, 1, 2), coefficients

    in_specs = (
        P("grp", "sub", None, None),
        P("grp", "sub", None, None, None, None),
        P("grp", "sub", None, None),
        P("grp", "sub"),
        P("grp", "sub", None, None),
        P("grp", "sub", None),
        P("grp", "sub", None, None, None),
        P("grp", "sub", None, None),
        P("grp", "sub", None, None, None),
        P("grp", "sub", None),
    )
    out_specs = (P("grp", "sub", None, None), P("grp", "sub", None, None), P("grp", "sub", None))
    return jax.shard_map(body, mesh=mesh, in_specs=in_specs, out_specs=out_specs, check_vma=False)
```

```python
import functools

import jax
import jax.numpy as jnp
from jax import lax
from jax.experimental import pallas as pl
from jax.experimental.pallas import tpu as pltpu
from jax.sharding import PartitionSpec as P

ITERS = 3
SWEEPS = 2
CSWEEPS = 2
LANES = 128

robin_weight = 1.0
omega_step = 0.2
highest = lax.Precision.HIGHEST
MESH = pl.DeviceIdType.MESH


def pick_lanes(field, index):
    rows = field.shape[0]
    parts = []
    for d in range(index.shape[1] // LANES):
        wanted = jnp.broadcast_to(index[:, d * LANES : (d + 1) * LANES], (rows, LANES))
        within = wanted & (LANES - 1)
        chunk = wanted >> (LANES.bit_length() - 1)
        out = None
        for s in range(field.shape[1] // LANES):
            got = jnp.take_along_axis(
                field[:, s * LANES : (s + 1) * LANES], within, axis=1, mode="promise_in_bounds"
            )
            out = got if out is None else jnp.where(chunk == s, got, out)
        parts.append(out)
    return jnp.concatenate(parts, axis=1) if len(parts) > 1 else parts[0]


def iota(shape, dim):
    return lax.broadcasted_iota(jnp.int32, shape, dim)


def kernel(
    groups,
    peers,
    load_hbm,
    couple_hbm,
    link_hbm,
    count_hbm,
    slot_hbm,
    pair_hbm,
    basis_hbm,
    inverse_hbm,
    block_hbm,
    coarse_link_hbm,
    trace_out,
    robin_out,
    coef_out,
    load_ref,
    couple_ref,
    link_ref,
    count_ref,
    slot_ref,
    pair_ref,
    basis_ref,
    inverse_ref,
    block_ref,
    coarse_link_ref,
    load_s,
    trace_s,
    robin_s,
    bx_s,
    couple_s,
    moved_s,
    kept_s,
    table_s,
    folded_s,
    slots_s,
    inside_s,
    owner_s,
    interface_s,
    start_s,
    coarse_send,
    coarse_recv,
    robin_send,
    robin_recv,
    coarse_send_sem,
    coarse_recv_sem,
    robin_send_sem,
    robin_recv_sem,
    input_sem,
):
    g, me = lax.axis_index("grp"), lax.axis_index("sub")
    trace_dim, faces = load_ref.shape[1], load_ref.shape[-1]
    rows = load_s.shape[0]
    cvec = inverse_ref.shape[-1]
    links = link_ref.shape[1]
    kc = coarse_link_ref.shape[-1]
    cap = slot_ref.shape[-1]
    slot_lanes = peers * cap

    def per_group(act):
        @pl.when(g > 0)
        def _():
            act(-1)

        @pl.when(g < groups - 1)
        def _():
            act(1)

        act(0)

    def targets(d):
        first = 1 if d == 0 else 0
        return [(g + d, lax.rem(me + off, peers)) for off in range(first, peers)]

    operands = (
        (count_hbm, count_ref),
        (load_hbm, load_ref),
        (link_hbm, link_ref),
        (slot_hbm, slot_ref),
        (pair_hbm, pair_ref),
        (couple_hbm, couple_ref),
        (inverse_hbm, inverse_ref),
        (basis_hbm, basis_ref),
        (block_hbm, block_ref),
        (coarse_link_hbm, coarse_link_ref),
    )
    fetches = [
        pltpu.make_async_copy(src, dst, input_sem.at[i]) for i, (src, dst) in enumerate(operands)
    ]
    for fetch in fetches:
        fetch.start()
    barrier = pltpu.get_barrier_semaphore()

    def greet(d):
        for device in targets(d):
            pl.semaphore_signal(barrier, inc=1, device_id=device, device_id_type=MESH)

    per_group(greet)

    for fetch in fetches[:5]:
        fetch.wait()
    live = (iota((1, faces), 1) < count_ref[0, 0]).astype(jnp.float32)
    load_s[...] = jnp.zeros_like(load_s)
    for a in range(trace_dim):
        load_s[a : a + 1, :] = load_ref[0, a] * live
    bx_s[...] = jnp.zeros_like(bx_s)
    moved_s[...] = jnp.zeros_like(moved_s)

    def unpack(a, carry):
        for s in range(faces // LANES):
            for k in range(links + 1):
                couple_s[s, a, (k + 1) * rows - 8 : (k + 1) * rows, :] = jnp.zeros((8, LANES), jnp.float32)
        for b in range(trace_dim):
            blocks = couple_ref[0, 0, a, b].astype(jnp.float32)
            for s in range(faces // LANES):
                couple_s[s, a, pl.ds(b, links + 1, stride=rows), :] = blocks[:, s * LANES : (s + 1) * LANES]
        return carry

    coarse_send[...] = jnp.zeros_like(coarse_send)
    slots_s[...] = jnp.zeros_like(slots_s)
    inside = jnp.zeros((1, faces), jnp.float32)
    owner = jnp.full((1, faces), -1.0, jnp.float32)
    eye_slots = iota((cap, cap), 0) == iota((cap, cap), 1)
    face_ids = iota((cap, faces), 1).astype(jnp.float32)
    place = iota((cap, faces), 0)
    for j in range(peers):
        slot_row = slot_ref[0, 0, j : j + 1, :]
        slots_s[:, j * cap : (j + 1) * cap] = slot_row
        as_float = jnp.broadcast_to(slot_row.astype(jnp.float32), (cap, cap))
        column = jnp.sum(jnp.where(eye_slots, as_float, 0.0), axis=1, keepdims=True)
        hit = (column == face_ids) & (place < pair_ref[0, 0, j])
        found = jnp.max(jnp.where(hit, place.astype(jnp.float32), -1.0), axis=0, keepdims=True)
        inside = jnp.where(found >= 0.0, found, inside)
        owner = jnp.where(found >= 0.0, float(j), owner)
    interface_s[...] = jnp.where(owner >= 0.0, 1.0, 0.0)
    inside_s[...] = inside.astype(jnp.int32)
    owner_s[...] = owner.astype(jnp.int32)
    robin_s[...] = jnp.zeros_like(robin_s)
    trace_s[...] = omega_step * load_s[...]
    eye = iota((cvec, cvec), 0) == iota((cvec, cvec), 1)

    fetches[5].wait()
    lax.fori_loop(0, trace_dim, unpack, 0)
    def apply(x):
        stacked = [x] + [
            pick_lanes(x, link_ref[0, k]) for k in range(links)
        ]
        for s in range(faces // LANES):
            lanes = slice(s * LANES, (s + 1) * LANES)
            for a in range(trace_dim):
                total = couple_s[s, a, 0:rows, :] * stacked[0][:, lanes]
                for k in range(1, links + 1):
                    total = total + couple_s[s, a, k * rows : (k + 1) * rows, :] * stacked[k][:, lanes]
                bx_s[a : a + 1, lanes] = jnp.sum(total, axis=0, keepdims=True)
        return live * (bx_s[...] + robin_weight * interface_s[...] * x)

    def right_side():
        return load_s[...] + live * robin_s[...]

    def sweep(x, bx):
        return x + omega_step * (right_side() - bx)

    def as_row(column):
        return jnp.sum(jnp.where(eye, column, 0.0), axis=0, keepdims=True)

    def send_row(t, r, row):
        coarse_send[t, r, :, 0:cvec] = row

        def push(d):
            for device in targets(d):
                pltpu.make_async_remote_copy(
                    src_ref=coarse_send.at[t, r],
                    dst_ref=coarse_recv.at[t, r, (1 - d) * peers + me],
                    send_sem=coarse_send_sem.at[t, r, 1 + d],
                    recv_sem=coarse_recv_sem.at[t, r, 1 - d],
                    device_id=device,
                    device_id_type=MESH,
                ).start()

        per_group(push)

    def wait_rows(t, r, sems):
        def wait(d):
            n = peers - 1 if d == 0 else peers
            part = coarse_recv.at[t, r, pl.ds((1 + d) * peers, n)]
            pltpu.make_async_copy(part, part, sems.at[t, r, 1 + d]).wait()

        per_group(wait)

    def coupled(t, r):
        table_s[...] = coarse_recv[t, r]
        total = None
        for k in range(kc):
            position = coarse_link_ref[0, 0, k] - (g - 1) * peers
            position = jnp.minimum(jnp.maximum(position, 0), 3 * peers - 1)
            term = folded_s[k] * table_s[position][:, 0:cvec]
            total = term if total is None else total + term
        return jnp.sum(total, axis=1, keepdims=True)

    def robin_copy(t, off):
        to = lax.rem(me + off, peers)
        chunk = lax.div(to * cap, LANES)
        return pltpu.make_async_remote_copy(
            src_ref=robin_send.at[t, chunk],
            dst_ref=robin_recv.at[t, off - 1],
            send_sem=robin_send_sem.at[t, off - 1],
            recv_sem=robin_recv_sem.at[t, off - 1],
            device_id=(g, to),
            device_id_type=MESH,
        )

    def front():
        x = trace_s[...]
        for _ in range(SWEEPS - 1):
            x = sweep(x, apply(x))
        residual = right_side() - apply(x)
        trace_s[...] = x
        part = jnp.zeros((cvec, LANES), jnp.float32)
        for a in range(trace_dim):
            product = basis_ref[0, 0, a] * residual[a : a + 1, :]
            for s in range(faces // LANES):
                part = part + product[:, s * LANES : (s + 1) * LANES]
        restricted = jnp.sum(part, axis=1, keepdims=True)
        start = jnp.sum(inverse_ref[0, 0] * as_row(restricted), axis=1, keepdims=True)
        start_s[...] = jnp.broadcast_to(start, start_s.shape)

    def fold():
        for k in range(kc):
            folded_s[k] = jnp.dot(
                inverse_ref[0, 0],
                block_ref[0, 0, k],
                precision=highest,
                preferred_element_type=jnp.float32,
            )

    for fetch in fetches[6:]:
        fetch.wait()
    front()
    count = (peers - 1) + jnp.where(g > 0, peers, 0) + jnp.where(g < groups - 1, peers, 0)
    pl.semaphore_wait(barrier, count)

    def iteration(t, carry):
        start = start_s[:, 0:1]
        coef = start
        for r in range(CSWEEPS):
            send_row(t, r, as_row(coef))
            if r == 0:
                pl.when(t == 0)(fold)
            wait_rows(t, r, coarse_recv_sem)
            coef = start - coupled(t, r)
        coef_out[0] = as_row(coef)
        wide = jnp.broadcast_to(coef, (cvec, faces))
        for a in range(trace_dim):
            moved_s[a : a + 1, :] = jnp.sum(basis_ref[0, 0, a] * wide, axis=0, keepdims=True)
        x = trace_s[...] + live * moved_s[...]
        kept_s[...] = x
        outgoing = 2.0 * robin_weight * x - robin_s[...]
        sent = pick_lanes(outgoing, slots_s[...])
        for s in range(slots_s.shape[1] // LANES):
            robin_send[t, s] = sent[:, s * LANES : (s + 1) * LANES]
        for off in range(1, peers):
            robin_copy(t, off).start()
        bx = apply(x)
        base = lax.rem(me * cap, LANES)
        inside = inside_s[...] + base
        owner = owner_s[...]
        fresh = jnp.zeros((rows, faces), jnp.float32)
        for off in range(1, peers):
            robin_copy(t, off).wait_recv()
            source = lax.rem(me + peers - off, peers)
            got = pick_lanes(robin_recv[t, off - 1], inside)
            fresh = jnp.where(owner == source, got, fresh)
        robin_s[...] = fresh
        trace_s[...] = sweep(x, bx)
        pl.when(t < ITERS - 1)(front)
        for r in range(CSWEEPS):
            wait_rows(t, r, coarse_send_sem)
        for off in range(1, peers):
            robin_copy(t, off).wait_send()
        return carry

    lax.fori_loop(0, ITERS, iteration, 0)
    for a in range(trace_dim):
        trace_out[0, a] = kept_s[a : a + 1, :]
        robin_out[0, a] = robin_s[a : a + 1, :]


def hand_out(*refs):
    sems = refs[-1]
    count = len(refs) // 2
    copies = [pltpu.make_async_copy(refs[i], refs[count + i], sems.at[i]) for i in range(count)]
    for copy in copies:
        copy.start()
    for copy in copies:
        copy.wait()


def solution(mesh):
    groups, peers = mesh.shape["grp"], mesh.shape["sub"]

    def body(
        load,
        couple,
        face_link,
        face_count,
        slot_face,
        pair_count,
        basis,
        coarse_inverse,
        coarse_block,
        coarse_link,
    ):
        trace_dim, faces = load.shape[-2:]
        rows = -(-trace_dim // 8) * 8
        links = face_link.shape[-2]
        cvec = basis.shape[2]
        kc = coarse_link.shape[-1]
        cap = slot_face.shape[-1]
        chunks = -(-peers * cap // LANES)
        vmem, smem = pltpu.VMEM, pltpu.SMEM
        operands = (
            jnp.swapaxes(load, 1, 2),
            jnp.transpose(couple, (0, 1, 3, 4, 2, 5)),
            jnp.swapaxes(face_link, 1, 2),
            face_count,
            slot_face,
            pair_count,
            jnp.swapaxes(basis, 2, 3),
            coarse_inverse,
            coarse_block,
            coarse_link,
        )
        f32 = jnp.float32
        spec = lambda space: pl.BlockSpec(memory_space=space)
        results = pl.pallas_call(
            functools.partial(kernel, groups, peers),
            out_shape=(
                jax.ShapeDtypeStruct((1, trace_dim, 1, faces), f32),
                jax.ShapeDtypeStruct((1, trace_dim, 1, faces), f32),
                jax.ShapeDtypeStruct((1, 1, cvec), f32),
            ),
            in_specs=[spec(pltpu.HBM)] * len(operands),
            out_specs=(spec(vmem), spec(vmem), spec(vmem)),
            scratch_shapes=[
                space(x.shape, x.dtype)
                for x, space in zip(operands, (vmem, vmem, vmem, smem, vmem, smem, vmem, vmem, vmem, smem))
            ]
            + [
                vmem((rows, faces), f32),
                vmem((rows, faces), f32),
                vmem((rows, faces), f32),
                vmem((rows, faces), f32),
                vmem((faces // LANES, trace_dim, (links + 1) * rows, LANES), f32),
                vmem((rows, faces), f32),
                vmem((rows, faces), f32),
                vmem((3 * peers, 1, LANES), f32),
                vmem((kc, cvec, cvec), f32),
                vmem((1, chunks * LANES), jnp.int32),
                vmem((1, faces), jnp.int32),
                vmem((1, faces), jnp.int32),
                vmem((1, faces), f32),
                vmem((cvec, LANES), f32),
                vmem((ITERS, CSWEEPS, 1, LANES), f32),
                vmem((ITERS, CSWEEPS, 3 * peers, 1, LANES), f32),
                vmem((ITERS, chunks, rows, LANES), f32),
                vmem((ITERS, peers - 1, rows, LANES), f32),
                pltpu.SemaphoreType.DMA((ITERS, CSWEEPS, 3)),
                pltpu.SemaphoreType.DMA((ITERS, CSWEEPS, 3)),
                pltpu.SemaphoreType.DMA((ITERS, peers - 1)),
                pltpu.SemaphoreType.DMA((ITERS, peers - 1)),
                pltpu.SemaphoreType.DMA((len(operands),)),
            ],
            compiler_params=pltpu.CompilerParams(
                collective_id=0, has_side_effects=True, vmem_limit_bytes=56 * 1024 * 1024
            ),
        )(*operands)
        trace_field, robin_data, coefficients = pl.pallas_call(
            hand_out,
            out_shape=tuple(jax.ShapeDtypeStruct(x.shape, x.dtype) for x in results),
            in_specs=[spec(pl.ANY)] * 3,
            out_specs=(spec(pl.ANY),) * 3,
            scratch_shapes=[pltpu.SemaphoreType.DMA((3,))],
        )(*results)
        return jnp.swapaxes(trace_field, 1, 2), jnp.swapaxes(robin_data, 1, 2), coefficients

    in_specs = (
        P("grp", "sub", None, None),
        P("grp", "sub", None, None, None, None),
        P("grp", "sub", None, None),
        P("grp", "sub"),
        P("grp", "sub", None, None),
        P("grp", "sub", None),
        P("grp", "sub", None, None, None),
        P("grp", "sub", None, None),
        P("grp", "sub", None, None, None),
        P("grp", "sub", None),
    )
    out_specs = (P("grp", "sub", None, None), P("grp", "sub", None, None), P("grp", "sub", None))
    return jax.shard_map(body, mesh=mesh, in_specs=in_specs, out_specs=out_specs, check_vma=False)
```

```python
import functools

import jax
import jax.numpy as jnp
from jax import lax
from jax.experimental import pallas as pl
from jax.experimental.pallas import tpu as pltpu
from jax.sharding import PartitionSpec as P

ITERS = 3
SWEEPS = 2
CSWEEPS = 2
LANES = 128

robin_weight = 1.0
omega_step = 0.2
highest = lax.Precision.HIGHEST
MESH = pl.DeviceIdType.MESH


def pick_lanes(field, index):
    rows = field.shape[0]
    parts = []
    for d in range(index.shape[1] // LANES):
        wanted = jnp.broadcast_to(index[:, d * LANES : (d + 1) * LANES], (rows, LANES))
        within = wanted & (LANES - 1)
        chunk = wanted >> (LANES.bit_length() - 1)
        out = None
        for s in range(field.shape[1] // LANES):
            got = jnp.take_along_axis(
                field[:, s * LANES : (s + 1) * LANES], within, axis=1, mode="promise_in_bounds"
            )
            out = got if out is None else jnp.where(chunk == s, got, out)
        parts.append(out)
    return jnp.concatenate(parts, axis=1) if len(parts) > 1 else parts[0]


def iota(shape, dim):
    return lax.broadcasted_iota(jnp.int32, shape, dim)


def kernel(
    groups,
    peers,
    load_hbm,
    couple_hbm,
    link_hbm,
    count_hbm,
    slot_hbm,
    pair_hbm,
    basis_hbm,
    inverse_hbm,
    block_hbm,
    coarse_link_hbm,
    trace_out,
    robin_out,
    coef_out,
    load_ref,
    couple_ref,
    link_ref,
    count_ref,
    slot_ref,
    pair_ref,
    basis_ref,
    inverse_ref,
    block_ref,
    coarse_link_ref,
    load_s,
    trace_s,
    robin_s,
    stack_s,
    couple_s,
    moved_s,
    kept_s,
    table_s,
    folded_s,
    slots_s,
    inside_s,
    owner_s,
    interface_s,
    start_s,
    coarse_send,
    coarse_recv,
    robin_send,
    robin_recv,
    coarse_send_sem,
    coarse_recv_sem,
    robin_send_sem,
    robin_recv_sem,
    input_sem,
):
    g, me = lax.axis_index("grp"), lax.axis_index("sub")
    trace_dim, faces = load_ref.shape[1], load_ref.shape[-1]
    rows = load_s.shape[0]
    cvec = inverse_ref.shape[-1]
    links = link_ref.shape[1]
    kc = coarse_link_ref.shape[-1]
    cap = slot_ref.shape[-1]
    slot_lanes = peers * cap

    def per_group(act):
        @pl.when(g > 0)
        def _():
            act(-1)

        @pl.when(g < groups - 1)
        def _():
            act(1)

        act(0)

    def targets(d):
        first = 1 if d == 0 else 0
        return [(g + d, lax.rem(me + off, peers)) for off in range(first, peers)]

    operands = (
        (count_hbm, count_ref),
        (load_hbm, load_ref),
        (link_hbm, link_ref),
        (slot_hbm, slot_ref),
        (pair_hbm, pair_ref),
        (couple_hbm, couple_ref),
        (inverse_hbm, inverse_ref),
        (basis_hbm, basis_ref),
        (block_hbm, block_ref),
        (coarse_link_hbm, coarse_link_ref),
    )
    fetches = [
        pltpu.make_async_copy(src, dst, input_sem.at[i]) for i, (src, dst) in enumerate(operands)
    ]
    for fetch in fetches:
        fetch.start()
    barrier = pltpu.get_barrier_semaphore()

    def greet(d):
        for device in targets(d):
            pl.semaphore_signal(barrier, inc=1, device_id=device, device_id_type=MESH)

    per_group(greet)

    for fetch in fetches[:5]:
        fetch.wait()
    live = (iota((1, faces), 1) < count_ref[0, 0]).astype(jnp.float32)
    load_s[...] = jnp.zeros_like(load_s)
    for a in range(trace_dim):
        load_s[a : a + 1, :] = load_ref[0, a] * live
    moved_s[...] = jnp.zeros_like(moved_s)

    def unpack(b, carry):
        for s in range(faces // LANES):
            for k in range(links + 1):
                couple_s[s, b, (k + 1) * rows - 8 : (k + 1) * rows, :] = jnp.zeros((8, LANES), jnp.float32)
        for a in range(trace_dim):
            blocks = couple_ref[0, 0, a, b].astype(jnp.float32)
            for s in range(faces // LANES):
                couple_s[s, b, pl.ds(a, links + 1, stride=rows), :] = blocks[:, s * LANES : (s + 1) * LANES]
        return carry

    coarse_send[...] = jnp.zeros_like(coarse_send)
    slots_s[...] = jnp.zeros_like(slots_s)
    inside = jnp.zeros((1, faces), jnp.float32)
    owner = jnp.full((1, faces), -1.0, jnp.float32)
    eye_slots = iota((cap, cap), 0) == iota((cap, cap), 1)
    face_ids = iota((cap, faces), 1).astype(jnp.float32)
    place = iota((cap, faces), 0)
    for j in range(peers):
        slot_row = slot_ref[0, 0, j : j + 1, :]
        slots_s[:, j * cap : (j + 1) * cap] = slot_row
        as_float = jnp.broadcast_to(slot_row.astype(jnp.float32), (cap, cap))
        column = jnp.sum(jnp.where(eye_slots, as_float, 0.0), axis=1, keepdims=True)
        hit = (column == face_ids) & (place < pair_ref[0, 0, j])
        found = jnp.max(jnp.where(hit, place.astype(jnp.float32), -1.0), axis=0, keepdims=True)
        inside = jnp.where(found >= 0.0, found, inside)
        owner = jnp.where(found >= 0.0, float(j), owner)
    interface_s[...] = jnp.where(owner >= 0.0, 1.0, 0.0)
    inside_s[...] = inside.astype(jnp.int32)
    owner_s[...] = owner.astype(jnp.int32)
    robin_s[...] = jnp.zeros_like(robin_s)
    trace_s[...] = omega_step * load_s[...]
    eye = iota((cvec, cvec), 0) == iota((cvec, cvec), 1)

    fetches[5].wait()
    lax.fori_loop(0, trace_dim, unpack, 0)
    def apply(x):
        stack_s[0] = x
        for k in range(links):
            stack_s[k + 1] = pick_lanes(x, link_ref[0, k])
        chunks = []
        for s in range(faces // LANES):
            lanes = slice(s * LANES, (s + 1) * LANES)
            totals = []
            for k in range(links + 1):
                total = None
                for b in range(trace_dim):
                    term = couple_s[s, b, k * rows : (k + 1) * rows, :] * stack_s[k, b : b + 1, lanes]
                    total = term if total is None else total + term
                totals.append(total)
            chunks.append(functools.reduce(jnp.add, totals))
        product = jnp.concatenate(chunks, axis=1)
        return live * (product + robin_weight * interface_s[...] * x)

    def right_side():
        return load_s[...] + live * robin_s[...]

    def sweep(x, bx):
        return x + omega_step * (right_side() - bx)

    def as_row(column):
        return jnp.sum(jnp.where(eye, column, 0.0), axis=0, keepdims=True)

    def send_row(t, r, row):
        coarse_send[t, r, :, 0:cvec] = row

        def push(d):
            for device in targets(d):
                pltpu.make_async_remote_copy(
                    src_ref=coarse_send.at[t, r],
                    dst_ref=coarse_recv.at[t, r, (1 - d) * peers + me],
                    send_sem=coarse_send_sem.at[t, r, 1 + d],
                    recv_sem=coarse_recv_sem.at[t, r, 1 - d],
                    device_id=device,
                    device_id_type=MESH,
                ).start()

        per_group(push)

    def wait_rows(t, r, sems):
        def wait(d):
            n = peers - 1 if d == 0 else peers
            part = coarse_recv.at[t, r, pl.ds((1 + d) * peers, n)]
            pltpu.make_async_copy(part, part, sems.at[t, r, 1 + d]).wait()

        per_group(wait)

    def coupled(t, r):
        table_s[...] = coarse_recv[t, r]
        total = None
        for k in range(kc):
            position = coarse_link_ref[0, 0, k] - (g - 1) * peers
            position = jnp.minimum(jnp.maximum(position, 0), 3 * peers - 1)
            term = folded_s[k] * table_s[position][:, 0:cvec]
            total = term if total is None else total + term
        return jnp.sum(total, axis=1, keepdims=True)

    def robin_copy(t, off):
        to = lax.rem(me + off, peers)
        chunk = lax.div(to * cap, LANES)
        return pltpu.make_async_remote_copy(
            src_ref=robin_send.at[t, chunk],
            dst_ref=robin_recv.at[t, off - 1],
            send_sem=robin_send_sem.at[t, off - 1],
            recv_sem=robin_recv_sem.at[t, off - 1],
            device_id=(g, to),
            device_id_type=MESH,
        )

    def front():
        x = trace_s[...]
        for _ in range(SWEEPS - 1):
            x = sweep(x, apply(x))
        residual = right_side() - apply(x)
        trace_s[...] = x
        part = jnp.zeros((cvec, LANES), jnp.float32)
        for a in range(trace_dim):
            product = basis_ref[0, 0, a] * residual[a : a + 1, :]
            for s in range(faces // LANES):
                part = part + product[:, s * LANES : (s + 1) * LANES]
        restricted = jnp.sum(part, axis=1, keepdims=True)
        start = jnp.sum(inverse_ref[0, 0] * as_row(restricted), axis=1, keepdims=True)
        start_s[...] = jnp.broadcast_to(start, start_s.shape)

    def fold():
        for k in range(kc):
            folded_s[k] = jnp.dot(
                inverse_ref[0, 0],
                block_ref[0, 0, k],
                precision=highest,
                preferred_element_type=jnp.float32,
            )

    for fetch in fetches[6:]:
        fetch.wait()
    front()
    count = (peers - 1) + jnp.where(g > 0, peers, 0) + jnp.where(g < groups - 1, peers, 0)
    pl.semaphore_wait(barrier, count)

    def iteration(t, carry):
        start = start_s[:, 0:1]
        coef = start
        for r in range(CSWEEPS):
            send_row(t, r, as_row(coef))
            if r == 0:
                pl.when(t == 0)(fold)
            wait_rows(t, r, coarse_recv_sem)
            coef = start - coupled(t, r)
        coef_out[0] = as_row(coef)
        wide = jnp.broadcast_to(coef, (cvec, faces))
        for a in range(trace_dim):
            moved_s[a : a + 1, :] = jnp.sum(basis_ref[0, 0, a] * wide, axis=0, keepdims=True)
        x = trace_s[...] + live * moved_s[...]
        kept_s[...] = x
        outgoing = 2.0 * robin_weight * x - robin_s[...]
        sent = pick_lanes(outgoing, slots_s[...])
        for s in range(slots_s.shape[1] // LANES):
            robin_send[t, s] = sent[:, s * LANES : (s + 1) * LANES]
        for off in range(1, peers):
            robin_copy(t, off).start()
        bx = apply(x)
        base = lax.rem(me * cap, LANES)
        inside = inside_s[...] + base
        owner = owner_s[...]
        fresh = jnp.zeros((rows, faces), jnp.float32)
        for off in range(1, peers):
            robin_copy(t, off).wait_recv()
            source = lax.rem(me + peers - off, peers)
            got = pick_lanes(robin_recv[t, off - 1], inside)
            fresh = jnp.where(owner == source, got, fresh)
        robin_s[...] = fresh
        trace_s[...] = sweep(x, bx)
        pl.when(t < ITERS - 1)(front)
        for r in range(CSWEEPS):
            wait_rows(t, r, coarse_send_sem)
        for off in range(1, peers):
            robin_copy(t, off).wait_send()
        return carry

    lax.fori_loop(0, ITERS, iteration, 0)
    for a in range(trace_dim):
        trace_out[0, a] = kept_s[a : a + 1, :]
        robin_out[0, a] = robin_s[a : a + 1, :]


def hand_out(*refs):
    sems = refs[-1]
    count = len(refs) // 2
    copies = [pltpu.make_async_copy(refs[i], refs[count + i], sems.at[i]) for i in range(count)]
    for copy in copies:
        copy.start()
    for copy in copies:
        copy.wait()


def solution(mesh):
    groups, peers = mesh.shape["grp"], mesh.shape["sub"]

    def body(
        load,
        couple,
        face_link,
        face_count,
        slot_face,
        pair_count,
        basis,
        coarse_inverse,
        coarse_block,
        coarse_link,
    ):
        trace_dim, faces = load.shape[-2:]
        rows = -(-trace_dim // 8) * 8
        links = face_link.shape[-2]
        cvec = basis.shape[2]
        kc = coarse_link.shape[-1]
        cap = slot_face.shape[-1]
        chunks = -(-peers * cap // LANES)
        vmem, smem = pltpu.VMEM, pltpu.SMEM
        operands = (
            jnp.swapaxes(load, 1, 2),
            jnp.transpose(couple, (0, 1, 3, 4, 2, 5)),
            jnp.swapaxes(face_link, 1, 2),
            face_count,
            slot_face,
            pair_count,
            jnp.swapaxes(basis, 2, 3),
            coarse_inverse,
            coarse_block,
            coarse_link,
        )
        f32 = jnp.float32
        spec = lambda space: pl.BlockSpec(memory_space=space)
        results = pl.pallas_call(
            functools.partial(kernel, groups, peers),
            out_shape=(
                jax.ShapeDtypeStruct((1, trace_dim, 1, faces), f32),
                jax.ShapeDtypeStruct((1, trace_dim, 1, faces), f32),
                jax.ShapeDtypeStruct((1, 1, cvec), f32),
            ),
            in_specs=[spec(pltpu.HBM)] * len(operands),
            out_specs=(spec(vmem), spec(vmem), spec(vmem)),
            scratch_shapes=[
                space(x.shape, x.dtype)
                for x, space in zip(operands, (vmem, vmem, vmem, smem, vmem, smem, vmem, vmem, vmem, smem))
            ]
            + [
                vmem((rows, faces), f32),
                vmem((rows, faces), f32),
                vmem((rows, faces), f32),
                vmem((links + 1, rows, faces), f32),
                vmem((faces // LANES, trace_dim, (links + 1) * rows, LANES), f32),
                vmem((rows, faces), f32),
                vmem((rows, faces), f32),
                vmem((3 * peers, 1, LANES), f32),
                vmem((kc, cvec, cvec), f32),
                vmem((1, chunks * LANES), jnp.int32),
                vmem((1, faces), jnp.int32),
                vmem((1, faces), jnp.int32),
                vmem((1, faces), f32),
                vmem((cvec, LANES), f32),
                vmem((ITERS, CSWEEPS, 1, LANES), f32),
                vmem((ITERS, CSWEEPS, 3 * peers, 1, LANES), f32),
                vmem((ITERS, chunks, rows, LANES), f32),
                vmem((ITERS, peers - 1, rows, LANES), f32),
                pltpu.SemaphoreType.DMA((ITERS, CSWEEPS, 3)),
                pltpu.SemaphoreType.DMA((ITERS, CSWEEPS, 3)),
                pltpu.SemaphoreType.DMA((ITERS, peers - 1)),
                pltpu.SemaphoreType.DMA((ITERS, peers - 1)),
                pltpu.SemaphoreType.DMA((len(operands),)),
            ],
            compiler_params=pltpu.CompilerParams(
                collective_id=0, has_side_effects=True, vmem_limit_bytes=24 * 1024 * 1024
            ),
        )(*operands)
        trace_field, robin_data, coefficients = pl.pallas_call(
            hand_out,
            out_shape=tuple(jax.ShapeDtypeStruct(x.shape, x.dtype) for x in results),
            in_specs=[spec(vmem)] * 3,
            out_specs=(spec(pl.ANY),) * 3,
            scratch_shapes=[pltpu.SemaphoreType.DMA((3,))],
        )(*results)
        return jnp.swapaxes(trace_field, 1, 2), jnp.swapaxes(robin_data, 1, 2), coefficients

    in_specs = (
        P("grp", "sub", None, None),
        P("grp", "sub", None, None, None, None),
        P("grp", "sub", None, None),
        P("grp", "sub"),
        P("grp", "sub", None, None),
        P("grp", "sub", None),
        P("grp", "sub", None, None, None),
        P("grp", "sub", None, None),
        P("grp", "sub", None, None, None),
        P("grp", "sub", None),
    )
    out_specs = (P("grp", "sub", None, None), P("grp", "sub", None, None), P("grp", "sub", None))
    return jax.shard_map(body, mesh=mesh, in_specs=in_specs, out_specs=out_specs, check_vma=False)
```

```python
import functools

import jax
import jax.numpy as jnp
from jax import lax
from jax.experimental import pallas as pl
from jax.experimental.pallas import tpu as pltpu
from jax.sharding import PartitionSpec as P

ITERS = 3
SWEEPS = 2
CSWEEPS = 2
LANES = 128

robin_weight = 1.0
omega_step = 0.2
highest = lax.Precision.HIGHEST
MESH = pl.DeviceIdType.MESH


def pick_lanes(field, index):
    rows = field.shape[0]
    parts = []
    for d in range(index.shape[1] // LANES):
        wanted = jnp.broadcast_to(index[:, d * LANES : (d + 1) * LANES], (rows, LANES))
        within = wanted & (LANES - 1)
        chunk = wanted >> (LANES.bit_length() - 1)
        out = None
        for s in range(field.shape[1] // LANES):
            got = jnp.take_along_axis(
                field[:, s * LANES : (s + 1) * LANES], within, axis=1, mode="promise_in_bounds"
            )
            out = got if out is None else jnp.where(chunk == s, got, out)
        parts.append(out)
    return jnp.concatenate(parts, axis=1) if len(parts) > 1 else parts[0]


def iota(shape, dim):
    return lax.broadcasted_iota(jnp.int32, shape, dim)


def kernel(
    groups,
    peers,
    load_hbm,
    couple_hbm,
    link_hbm,
    count_hbm,
    slot_hbm,
    pair_hbm,
    basis_hbm,
    inverse_hbm,
    block_hbm,
    coarse_link_hbm,
    trace_out,
    robin_out,
    coef_out,
    load_ref,
    couple_ref,
    link_ref,
    count_ref,
    slot_ref,
    pair_ref,
    basis_ref,
    inverse_ref,
    block_ref,
    coarse_link_ref,
    load_s,
    trace_s,
    robin_s,
    stack_s,
    couple_s,
    moved_s,
    kept_s,
    table_s,
    folded_s,
    slots_s,
    inside_s,
    owner_s,
    interface_s,
    start_s,
    coef_s,
    coarse_send,
    coarse_recv,
    robin_send,
    robin_recv,
    coarse_send_sem,
    coarse_recv_sem,
    robin_send_sem,
    robin_recv_sem,
    input_sem,
):
    g, me = lax.axis_index("grp"), lax.axis_index("sub")
    trace_dim, faces = load_ref.shape[1], load_ref.shape[-1]
    rows = load_s.shape[0]
    cvec = inverse_ref.shape[-1]
    links = link_ref.shape[1]
    kc = coarse_link_ref.shape[-1]
    cap = slot_ref.shape[-1]
    slot_lanes = peers * cap

    def per_group(act):
        @pl.when(g > 0)
        def _():
            act(-1)

        @pl.when(g < groups - 1)
        def _():
            act(1)

        act(0)

    def after(off):
        return jnp.where(me + off >= peers, me + off - peers, me + off)

    def targets(d):
        first = 1 if d == 0 else 0
        return [(g + d, after(off)) for off in range(first, peers)]

    operands = (
        (count_hbm, count_ref),
        (load_hbm, load_ref),
        (link_hbm, link_ref),
        (slot_hbm, slot_ref),
        (pair_hbm, pair_ref),
        (couple_hbm, couple_ref),
        (inverse_hbm, inverse_ref),
        (basis_hbm, basis_ref),
        (block_hbm, block_ref),
        (coarse_link_hbm, coarse_link_ref),
    )
    fetches = [
        pltpu.make_async_copy(src, dst, input_sem.at[i]) for i, (src, dst) in enumerate(operands)
    ]
    for fetch in fetches:
        fetch.start()
    barrier = pltpu.get_barrier_semaphore()

    def greet(d):
        for device in targets(d):
            pl.semaphore_signal(barrier, inc=1, device_id=device, device_id_type=MESH)

    per_group(greet)

    for fetch in fetches[:5]:
        fetch.wait()
    live = (iota((1, faces), 1) < count_ref[0, 0]).astype(jnp.float32)
    load_s[...] = jnp.zeros_like(load_s)
    for a in range(trace_dim):
        load_s[a : a + 1, :] = load_ref[0, a] * live
    moved_s[...] = jnp.zeros_like(moved_s)

    def unpack(b, carry):
        for s in range(faces // LANES):
            for k in range(links + 1):
                couple_s[s, b, (k + 1) * rows - 8 : (k + 1) * rows, :] = jnp.zeros((8, LANES), jnp.float32)
        for a in range(trace_dim):
            blocks = couple_ref[0, 0, a, b].astype(jnp.float32)
            for s in range(faces // LANES):
                couple_s[s, b, pl.ds(a, links + 1, stride=rows), :] = blocks[:, s * LANES : (s + 1) * LANES]
        return carry

    coarse_send[...] = jnp.zeros_like(coarse_send)
    slots_s[...] = jnp.zeros_like(slots_s)
    inside = jnp.zeros((1, faces), jnp.float32)
    owner = jnp.full((1, faces), -1.0, jnp.float32)
    eye_slots = iota((cap, cap), 0) == iota((cap, cap), 1)
    face_ids = iota((cap, faces), 1).astype(jnp.float32)
    place = iota((cap, faces), 0)
    for j in range(peers):
        slot_row = slot_ref[0, 0, j : j + 1, :]
        slots_s[:, j * cap : (j + 1) * cap] = slot_row
        as_float = jnp.broadcast_to(slot_row.astype(jnp.float32), (cap, cap))
        column = jnp.sum(jnp.where(eye_slots, as_float, 0.0), axis=1, keepdims=True)
        hit = (column == face_ids) & (place < pair_ref[0, 0, j])
        found = jnp.max(jnp.where(hit, place.astype(jnp.float32), -1.0), axis=0, keepdims=True)
        inside = jnp.where(found >= 0.0, found, inside)
        owner = jnp.where(found >= 0.0, float(j), owner)
    interface_s[...] = jnp.where(owner >= 0.0, 1.0, 0.0)
    inside_s[...] = inside.astype(jnp.int32)
    owner_s[...] = owner.astype(jnp.int32)
    robin_s[...] = jnp.zeros_like(robin_s)
    trace_s[...] = omega_step * load_s[...]
    eye = iota((cvec, cvec), 0) == iota((cvec, cvec), 1)

    fetches[5].wait()
    lax.fori_loop(0, trace_dim, unpack, 0)
    count = (peers - 1) + jnp.where(g > 0, peers, 0) + jnp.where(g < groups - 1, peers, 0)

    def apply(x):
        stack_s[0] = x
        for k in range(links):
            stack_s[k + 1] = pick_lanes(x, link_ref[0, k])
        chunks = []
        for s in range(faces // LANES):
            lanes = slice(s * LANES, (s + 1) * LANES)
            totals = []
            for k in range(links + 1):
                total = None
                for b in range(trace_dim):
                    term = couple_s[s, b, k * rows : (k + 1) * rows, :] * stack_s[k, b : b + 1, lanes]
                    total = term if total is None else total + term
                totals.append(total)
            chunks.append(functools.reduce(jnp.add, totals))
        product = jnp.concatenate(chunks, axis=1)
        return live * (product + robin_weight * interface_s[...] * x)

    def right_side():
        return load_s[...] + live * robin_s[...]

    def sweep(x, bx):
        return x + omega_step * (right_side() - bx)

    def as_row(column):
        return jnp.sum(jnp.where(eye, column, 0.0), axis=0, keepdims=True)

    def send_row(t, r, row):
        coarse_send[t, r, :, 0:cvec] = row

        def push(d):
            for device in targets(d):
                pltpu.make_async_remote_copy(
                    src_ref=coarse_send.at[t, r],
                    dst_ref=coarse_recv.at[t, r, (1 - d) * peers + me],
                    send_sem=coarse_send_sem.at[t, r, 1 + d],
                    recv_sem=coarse_recv_sem.at[t, r, 1 - d],
                    device_id=device,
                    device_id_type=MESH,
                ).start()

        per_group(push)

    def wait_rows(t, r, sems):
        def wait(d):
            n = peers - 1 if d == 0 else peers
            part = coarse_recv.at[t, r, pl.ds((1 + d) * peers, n)]
            pltpu.make_async_copy(part, part, sems.at[t, r, 1 + d]).wait()

        per_group(wait)

    def coupled(t, r):
        table_s[...] = coarse_recv[t, r]
        total = None
        for k in range(kc):
            position = coarse_link_ref[0, 0, k] - (g - 1) * peers
            position = jnp.minimum(jnp.maximum(position, 0), 3 * peers - 1)
            term = folded_s[k] * table_s[position][:, 0:cvec]
            total = term if total is None else total + term
        return jnp.sum(total, axis=1, keepdims=True)

    def robin_copy(t, off):
        to = after(off)
        chunk = lax.div(to * cap, LANES)
        return pltpu.make_async_remote_copy(
            src_ref=robin_send.at[t, chunk],
            dst_ref=robin_recv.at[t, off - 1],
            send_sem=robin_send_sem.at[t, off - 1],
            recv_sem=robin_recv_sem.at[t, off - 1],
            device_id=(g, to),
            device_id_type=MESH,
        )

    def fold():
        for k in range(kc):
            folded_s[k] = jnp.dot(
                inverse_ref[0, 0],
                block_ref[0, 0, k],
                precision=highest,
                preferred_element_type=jnp.float32,
            )

    def relax(bx):
        trace_s[...] = sweep(trace_s[...], bx)

    def coarse(t, bx):
        residual = right_side() - bx
        part = jnp.zeros((cvec, LANES), jnp.float32)
        for a in range(trace_dim):
            product = basis_ref[0, 0, a] * residual[a : a + 1, :]
            for s in range(faces // LANES):
                part = part + product[:, s * LANES : (s + 1) * LANES]
        restricted = jnp.sum(part, axis=1, keepdims=True)
        start = jnp.sum(inverse_ref[0, 0] * as_row(restricted), axis=1, keepdims=True)
        start_s[...] = jnp.broadcast_to(start, start_s.shape)
        coef_s[...] = start_s[...]

        def exchange(r, carry):
            send_row(t, r, as_row(coef_s[:, 0:cvec]))
            pl.when((t == 0) & (r == 0))(fold)
            wait_rows(t, r, coarse_recv_sem)
            coef_s[...] = start_s[...] - coupled(t, r)
            return carry

        lax.fori_loop(0, CSWEEPS, exchange, 0)
        coef_out[0] = as_row(coef_s[:, 0:cvec])
        wide = jnp.concatenate([coef_s[...]] * (faces // LANES), axis=1)
        for a in range(trace_dim):
            moved_s[a : a + 1, :] = jnp.sum(basis_ref[0, 0, a] * wide, axis=0, keepdims=True)
        x = trace_s[...] + live * moved_s[...]
        trace_s[...] = x
        kept_s[...] = x
        outgoing = 2.0 * robin_weight * x - robin_s[...]
        sent = pick_lanes(outgoing, slots_s[...])
        for s in range(slots_s.shape[1] // LANES):
            robin_send[t, s] = sent[:, s * LANES : (s + 1) * LANES]
        for off in range(1, peers):
            robin_copy(t, off).start()

    def settle(t, bx):
        base = lax.rem(me * cap, LANES)
        inside = inside_s[...] + base
        owner = owner_s[...]
        fresh = jnp.zeros((rows, faces), jnp.float32)
        for off in range(1, peers):
            robin_copy(t, off).wait_recv()
            source = after(peers - off)
            got = pick_lanes(robin_recv[t, off - 1], inside)
            fresh = jnp.where(owner == source, got, fresh)
        robin_s[...] = fresh
        trace_s[...] = sweep(trace_s[...], bx)
        for r in range(CSWEEPS):
            wait_rows(t, r, coarse_send_sem)
        for off in range(1, peers):
            robin_copy(t, off).wait_send()

    phases = SWEEPS + 1

    def step(n, carry):
        t = n // phases
        phase = n - t * phases
        bx = apply(trace_s[...])
        pl.when(phase < SWEEPS - 1)(lambda: relax(bx))

        @pl.when(n == SWEEPS - 1)
        def _():
            pl.semaphore_wait(barrier, count)
            for fetch in fetches[6:]:
                fetch.wait()

        pl.when(phase == SWEEPS - 1)(lambda: coarse(t, bx))
        pl.when(phase == SWEEPS)(lambda: settle(t, bx))
        return carry

    lax.fori_loop(0, ITERS * phases, step, 0)
    for a in range(trace_dim):
        trace_out[0, a] = kept_s[a : a + 1, :]
        robin_out[0, a] = robin_s[a : a + 1, :]


def solution(mesh):
    groups, peers = mesh.shape["grp"], mesh.shape["sub"]

    def body(
        load,
        couple,
        face_link,
        face_count,
        slot_face,
        pair_count,
        basis,
        coarse_inverse,
        coarse_block,
        coarse_link,
    ):
        trace_dim, faces = load.shape[-2:]
        rows = -(-trace_dim // 8) * 8
        links = face_link.shape[-2]
        cvec = basis.shape[2]
        kc = coarse_link.shape[-1]
        cap = slot_face.shape[-1]
        chunks = -(-peers * cap // LANES)
        vmem, smem = pltpu.VMEM, pltpu.SMEM
        operands = (
            jnp.swapaxes(load, 1, 2),
            jnp.transpose(couple, (0, 1, 3, 4, 2, 5)),
            jnp.swapaxes(face_link, 1, 2),
            face_count,
            slot_face,
            pair_count,
            jnp.swapaxes(basis, 2, 3),
            coarse_inverse,
            coarse_block,
            coarse_link,
        )
        f32 = jnp.float32
        spec = lambda space: pl.BlockSpec(memory_space=space)
        trace_field, robin_data, coefficients = pl.pallas_call(
            functools.partial(kernel, groups, peers),
            out_shape=(
                jax.ShapeDtypeStruct((1, trace_dim, 1, faces), f32),
                jax.ShapeDtypeStruct((1, trace_dim, 1, faces), f32),
                jax.ShapeDtypeStruct((1, 1, cvec), f32),
            ),
            in_specs=[spec(pltpu.HBM)] * len(operands),
            out_specs=(spec(vmem), spec(vmem), spec(vmem)),
            scratch_shapes=[
                space(x.shape, x.dtype)
                for x, space in zip(operands, (vmem, vmem, vmem, smem, vmem, smem, vmem, vmem, vmem, smem))
            ]
            + [
                vmem((rows, faces), f32),
                vmem((rows, faces), f32),
                vmem((rows, faces), f32),
                vmem((links + 1, rows, faces), f32),
                vmem((faces // LANES, trace_dim, (links + 1) * rows, LANES), f32),
                vmem((rows, faces), f32),
                vmem((rows, faces), f32),
                vmem((3 * peers, 1, LANES), f32),
                vmem((kc, cvec, cvec), f32),
                vmem((1, chunks * LANES), jnp.int32),
                vmem((1, faces), jnp.int32),
                vmem((1, faces), jnp.int32),
                vmem((1, faces), f32),
                vmem((cvec, LANES), f32),
                vmem((cvec, LANES), f32),
                vmem((ITERS, CSWEEPS, 1, LANES), f32),
                vmem((ITERS, CSWEEPS, 3 * peers, 1, LANES), f32),
                vmem((ITERS, chunks, rows, LANES), f32),
                vmem((ITERS, peers - 1, rows, LANES), f32),
                pltpu.SemaphoreType.DMA((ITERS, CSWEEPS, 3)),
                pltpu.SemaphoreType.DMA((ITERS, CSWEEPS, 3)),
                pltpu.SemaphoreType.DMA((ITERS, peers - 1)),
                pltpu.SemaphoreType.DMA((ITERS, peers - 1)),
                pltpu.SemaphoreType.DMA((len(operands),)),
            ],
            compiler_params=pltpu.CompilerParams(
                collective_id=0, has_side_effects=True, vmem_limit_bytes=56 * 1024 * 1024
            ),
        )(*operands)
        return jnp.swapaxes(trace_field, 1, 2), jnp.swapaxes(robin_data, 1, 2), coefficients

    in_specs = (
        P("grp", "sub", None, None),
        P("grp", "sub", None, None, None, None),
        P("grp", "sub", None, None),
        P("grp", "sub"),
        P("grp", "sub", None, None),
        P("grp", "sub", None),
        P("grp", "sub", None, None, None),
        P("grp", "sub", None, None),
        P("grp", "sub", None, None, None),
        P("grp", "sub", None),
    )
    out_specs = (P("grp", "sub", None, None), P("grp", "sub", None, None), P("grp", "sub", None))
    return jax.shard_map(body, mesh=mesh, in_specs=in_specs, out_specs=out_specs, check_vma=False)
```

```python
import functools

import jax
import jax.numpy as jnp
from jax import lax
from jax.experimental import pallas as pl
from jax.experimental.pallas import tpu as pltpu
from jax.sharding import PartitionSpec as P

ITERS = 3
SWEEPS = 2
CSWEEPS = 2
LANES = 128

robin_weight = 1.0
omega_step = 0.2
highest = lax.Precision.HIGHEST
MESH = pl.DeviceIdType.MESH


def pick_lanes(field, hot):
    pieces, rest = [], field
    for _ in range(3):
        piece = rest.astype(jnp.bfloat16)
        rest = rest - piece.astype(jnp.float32)
        pieces.append(piece)
    got = jnp.dot(jnp.concatenate(pieces, axis=0), hot, preferred_element_type=jnp.float32)
    rows = field.shape[0]
    return got[0:rows] + got[rows : 2 * rows] + got[2 * rows : 3 * rows]


def one_hot(index, count):
    return jnp.where(iota((count, index.shape[1]), 0) == index, 1.0, 0.0).astype(jnp.bfloat16)


def iota(shape, dim):
    return lax.broadcasted_iota(jnp.int32, shape, dim)


def kernel(
    groups,
    peers,
    load_hbm,
    couple_hbm,
    link_hbm,
    count_hbm,
    slot_hbm,
    pair_hbm,
    basis_hbm,
    inverse_hbm,
    block_hbm,
    coarse_link_hbm,
    trace_out,
    robin_out,
    coef_out,
    load_ref,
    couple_ref,
    link_ref,
    count_ref,
    slot_ref,
    pair_ref,
    basis_ref,
    inverse_ref,
    block_ref,
    coarse_link_ref,
    load_s,
    trace_s,
    robin_s,
    stack_s,
    couple_s,
    moved_s,
    kept_s,
    table_s,
    folded_s,
    slots_s,
    link_hot,
    out_hot,
    in_hot,
    interface_s,
    start_s,
    coef_s,
    coarse_send,
    coarse_recv,
    robin_send,
    robin_recv,
    coarse_send_sem,
    coarse_recv_sem,
    robin_send_sem,
    robin_recv_sem,
    input_sem,
):
    g, me = lax.axis_index("grp"), lax.axis_index("sub")
    trace_dim, faces = load_ref.shape[1], load_ref.shape[-1]
    rows = load_s.shape[0]
    cvec = inverse_ref.shape[-1]
    links = link_ref.shape[1]
    kc = coarse_link_ref.shape[-1]
    cap = slot_ref.shape[-1]
    slot_lanes = peers * cap

    def per_group(act):
        @pl.when(g > 0)
        def _():
            act(-1)

        @pl.when(g < groups - 1)
        def _():
            act(1)

        act(0)

    def after(off):
        return jnp.where(me + off >= peers, me + off - peers, me + off)

    def targets(d):
        first = 1 if d == 0 else 0
        return [(g + d, after(off)) for off in range(first, peers)]

    operands = (
        (count_hbm, count_ref),
        (load_hbm, load_ref),
        (link_hbm, link_ref),
        (slot_hbm, slot_ref),
        (pair_hbm, pair_ref),
        (couple_hbm, couple_ref),
        (inverse_hbm, inverse_ref),
        (basis_hbm, basis_ref),
        (block_hbm, block_ref),
        (coarse_link_hbm, coarse_link_ref),
    )
    fetches = [
        pltpu.make_async_copy(src, dst, input_sem.at[i]) for i, (src, dst) in enumerate(operands)
    ]
    for fetch in fetches:
        fetch.start()
    barrier = pltpu.get_barrier_semaphore()

    def greet(d):
        for device in targets(d):
            pl.semaphore_signal(barrier, inc=1, device_id=device, device_id_type=MESH)

    per_group(greet)

    for fetch in fetches[:5]:
        fetch.wait()
    live = (iota((1, faces), 1) < count_ref[0, 0]).astype(jnp.float32)
    load_s[...] = jnp.zeros_like(load_s)
    for a in range(trace_dim):
        load_s[a : a + 1, :] = load_ref[0, a] * live
    moved_s[...] = jnp.zeros_like(moved_s)

    def unpack(b, carry):
        for s in range(faces // LANES):
            for k in range(links + 1):
                couple_s[s, b, (k + 1) * rows - 8 : (k + 1) * rows, :] = jnp.zeros((8, LANES), jnp.float32)
        for a in range(trace_dim):
            blocks = couple_ref[0, 0, a, b].astype(jnp.float32)
            for s in range(faces // LANES):
                couple_s[s, b, pl.ds(a, links + 1, stride=rows), :] = blocks[:, s * LANES : (s + 1) * LANES]
        return carry

    coarse_send[...] = jnp.zeros_like(coarse_send)
    slots_s[...] = jnp.zeros_like(slots_s)
    inside = jnp.zeros((1, faces), jnp.float32)
    owner = jnp.full((1, faces), -1.0, jnp.float32)
    eye_slots = iota((cap, cap), 0) == iota((cap, cap), 1)
    face_ids = iota((cap, faces), 1).astype(jnp.float32)
    place = iota((cap, faces), 0)
    for j in range(peers):
        slot_row = slot_ref[0, 0, j : j + 1, :]
        slots_s[:, j * cap : (j + 1) * cap] = slot_row
        as_float = jnp.broadcast_to(slot_row.astype(jnp.float32), (cap, cap))
        column = jnp.sum(jnp.where(eye_slots, as_float, 0.0), axis=1, keepdims=True)
        hit = (column == face_ids) & (place < pair_ref[0, 0, j])
        found = jnp.max(jnp.where(hit, place.astype(jnp.float32), -1.0), axis=0, keepdims=True)
        inside = jnp.where(found >= 0.0, found, inside)
        owner = jnp.where(found >= 0.0, float(j), owner)
    interface_s[...] = jnp.where(owner >= 0.0, 1.0, 0.0)
    owner = owner.astype(jnp.int32)
    base = lax.rem(me * cap, LANES)
    for off in range(1, peers):
        rows_at = slice((off - 1) * LANES, off * LANES)
        wanted = jnp.where(owner == after(peers - off), inside.astype(jnp.int32) + base, -1)
        in_hot[rows_at, :] = one_hot(wanted, LANES)
    out_hot[...] = one_hot(slots_s[...], faces)
    for k in range(links):
        link_hot[:, k * faces : (k + 1) * faces] = one_hot(link_ref[0, k], faces)
    robin_s[...] = jnp.zeros_like(robin_s)
    trace_s[...] = omega_step * load_s[...]
    eye = iota((cvec, cvec), 0) == iota((cvec, cvec), 1)

    fetches[5].wait()
    lax.fori_loop(0, trace_dim, unpack, 0)
    count = (peers - 1) + jnp.where(g > 0, peers, 0) + jnp.where(g < groups - 1, peers, 0)

    def apply(x):
        stack_s[0] = x
        linked = pick_lanes(x, link_hot[...])
        for k in range(links):
            stack_s[k + 1] = linked[:, k * faces : (k + 1) * faces]
        chunks = []
        for s in range(faces // LANES):
            lanes = slice(s * LANES, (s + 1) * LANES)
            totals = []
            for k in range(links + 1):
                total = None
                for b in range(trace_dim):
                    term = couple_s[s, b, k * rows : (k + 1) * rows, :] * stack_s[k, b : b + 1, lanes]
                    total = term if total is None else total + term
                totals.append(total)
            chunks.append(functools.reduce(jnp.add, totals))
        product = jnp.concatenate(chunks, axis=1)
        return live * (product + robin_weight * interface_s[...] * x)

    def right_side():
        return load_s[...] + live * robin_s[...]

    def sweep(x, bx):
        return x + omega_step * (right_side() - bx)

    def as_row(column):
        return jnp.sum(jnp.where(eye, column, 0.0), axis=0, keepdims=True)

    def send_row(t, r, row):
        coarse_send[t, r, :, 0:cvec] = row

        def push(d):
            for device in targets(d):
                pltpu.make_async_remote_copy(
                    src_ref=coarse_send.at[t, r],
                    dst_ref=coarse_recv.at[t, r, (1 - d) * peers + me],
                    send_sem=coarse_send_sem.at[t, r, 1 + d],
                    recv_sem=coarse_recv_sem.at[t, r, 1 - d],
                    device_id=device,
                    device_id_type=MESH,
                ).start()

        per_group(push)

    def wait_rows(t, r, sems):
        def wait(d):
            n = peers - 1 if d == 0 else peers
            part = coarse_recv.at[t, r, pl.ds((1 + d) * peers, n)]
            pltpu.make_async_copy(part, part, sems.at[t, r, 1 + d]).wait()

        per_group(wait)

    def coupled(t, r):
        table_s[...] = coarse_recv[t, r]
        total = None
        for k in range(kc):
            position = coarse_link_ref[0, 0, k] - (g - 1) * peers
            position = jnp.minimum(jnp.maximum(position, 0), 3 * peers - 1)
            term = folded_s[k] * table_s[position][:, 0:cvec]
            total = term if total is None else total + term
        return jnp.sum(total, axis=1, keepdims=True)

    def robin_copy(t, off):
        to = after(off)
        chunk = lax.div(to * cap, LANES)
        return pltpu.make_async_remote_copy(
            src_ref=robin_send.at[t, chunk],
            dst_ref=robin_recv.at[t, off - 1],
            send_sem=robin_send_sem.at[t, off - 1],
            recv_sem=robin_recv_sem.at[t, off - 1],
            device_id=(g, to),
            device_id_type=MESH,
        )

    def fold():
        for k in range(kc):
            folded_s[k] = jnp.dot(
                inverse_ref[0, 0],
                block_ref[0, 0, k],
                precision=highest,
                preferred_element_type=jnp.float32,
            )

    def relax(bx):
        trace_s[...] = sweep(trace_s[...], bx)

    def coarse(t, bx):
        residual = right_side() - bx
        part = jnp.zeros((cvec, LANES), jnp.float32)
        for a in range(trace_dim):
            product = basis_ref[0, 0, a] * residual[a : a + 1, :]
            for s in range(faces // LANES):
                part = part + product[:, s * LANES : (s + 1) * LANES]
        restricted = jnp.sum(part, axis=1, keepdims=True)
        start = jnp.sum(inverse_ref[0, 0] * as_row(restricted), axis=1, keepdims=True)
        start_s[...] = jnp.broadcast_to(start, start_s.shape)
        coef_s[...] = start_s[...]

        def exchange(r, carry):
            send_row(t, r, as_row(coef_s[:, 0:cvec]))
            pl.when((t == 0) & (r == 0))(fold)
            wait_rows(t, r, coarse_recv_sem)
            coef_s[...] = start_s[...] - coupled(t, r)
            return carry

        lax.fori_loop(0, CSWEEPS, exchange, 0)
        coef_out[0] = as_row(coef_s[:, 0:cvec])
        wide = jnp.concatenate([coef_s[...]] * (faces // LANES), axis=1)
        for a in range(trace_dim):
            moved_s[a : a + 1, :] = jnp.sum(basis_ref[0, 0, a] * wide, axis=0, keepdims=True)
        x = trace_s[...] + live * moved_s[...]
        trace_s[...] = x
        kept_s[...] = x
        outgoing = 2.0 * robin_weight * x - robin_s[...]
        sent = pick_lanes(outgoing, out_hot[...])
        for s in range(slots_s.shape[1] // LANES):
            robin_send[t, s] = sent[:, s * LANES : (s + 1) * LANES]
        for off in range(1, peers):
            robin_copy(t, off).start()

    def settle(t, bx):
        for off in range(1, peers):
            robin_copy(t, off).wait_recv()
        arrived = jnp.concatenate([robin_recv[t, off - 1] for off in range(1, peers)], axis=1)
        fresh = pick_lanes(arrived, in_hot[...])
        robin_s[...] = fresh
        trace_s[...] = sweep(trace_s[...], bx)
        for r in range(CSWEEPS):
            wait_rows(t, r, coarse_send_sem)
        for off in range(1, peers):
            robin_copy(t, off).wait_send()

    phases = SWEEPS + 1

    def step(n, carry):
        t = n // phases
        phase = n - t * phases
        bx = apply(trace_s[...])
        pl.when(phase < SWEEPS - 1)(lambda: relax(bx))

        @pl.when(n == SWEEPS - 1)
        def _():
            pl.semaphore_wait(barrier, count)
            for fetch in fetches[6:]:
                fetch.wait()

        pl.when(phase == SWEEPS - 1)(lambda: coarse(t, bx))
        pl.when(phase == SWEEPS)(lambda: settle(t, bx))
        return carry

    lax.fori_loop(0, ITERS * phases, step, 0)
    for a in range(trace_dim):
        trace_out[0, a] = kept_s[a : a + 1, :]
        robin_out[0, a] = robin_s[a : a + 1, :]


def solution(mesh):
    groups, peers = mesh.shape["grp"], mesh.shape["sub"]

    def body(
        load,
        couple,
        face_link,
        face_count,
        slot_face,
        pair_count,
        basis,
        coarse_inverse,
        coarse_block,
        coarse_link,
    ):
        trace_dim, faces = load.shape[-2:]
        rows = -(-trace_dim // 8) * 8
        links = face_link.shape[-2]
        cvec = basis.shape[2]
        kc = coarse_link.shape[-1]
        cap = slot_face.shape[-1]
        chunks = -(-peers * cap // LANES)
        vmem, smem = pltpu.VMEM, pltpu.SMEM
        operands = (
            jnp.swapaxes(load, 1, 2),
            jnp.transpose(couple, (0, 1, 3, 4, 2, 5)),
            jnp.swapaxes(face_link, 1, 2),
            face_count,
            slot_face,
            pair_count,
            jnp.swapaxes(basis, 2, 3),
            coarse_inverse,
            coarse_block,
            coarse_link,
        )
        f32 = jnp.float32
        spec = lambda space: pl.BlockSpec(memory_space=space)
        trace_field, robin_data, coefficients = pl.pallas_call(
            functools.partial(kernel, groups, peers),
            out_shape=(
                jax.ShapeDtypeStruct((1, trace_dim, 1, faces), f32),
                jax.ShapeDtypeStruct((1, trace_dim, 1, faces), f32),
                jax.ShapeDtypeStruct((1, 1, cvec), f32),
            ),
            in_specs=[spec(pl.ANY)] * len(operands),
            out_specs=(spec(vmem), spec(vmem), spec(vmem)),
            scratch_shapes=[
                space(x.shape, x.dtype)
                for x, space in zip(operands, (vmem, vmem, vmem, smem, vmem, smem, vmem, vmem, vmem, smem))
            ]
            + [
                vmem((rows, faces), f32),
                vmem((rows, faces), f32),
                vmem((rows, faces), f32),
                vmem((links + 1, rows, faces), f32),
                vmem((faces // LANES, trace_dim, (links + 1) * rows, LANES), f32),
                vmem((rows, faces), f32),
                vmem((rows, faces), f32),
                vmem((3 * peers, 1, LANES), f32),
                vmem((kc, cvec, cvec), f32),
                vmem((1, chunks * LANES), jnp.int32),
                vmem((faces, links * faces), jnp.bfloat16),
                vmem((faces, chunks * LANES), jnp.bfloat16),
                vmem(((peers - 1) * LANES, faces), jnp.bfloat16),
                vmem((1, faces), f32),
                vmem((cvec, LANES), f32),
                vmem((cvec, LANES), f32),
                vmem((ITERS, CSWEEPS, 1, LANES), f32),
                vmem((ITERS, CSWEEPS, 3 * peers, 1, LANES), f32),
                vmem((ITERS, chunks, rows, LANES), f32),
                vmem((ITERS, peers - 1, rows, LANES), f32),
                pltpu.SemaphoreType.DMA((ITERS, CSWEEPS, 3)),
                pltpu.SemaphoreType.DMA((ITERS, CSWEEPS, 3)),
                pltpu.SemaphoreType.DMA((ITERS, peers - 1)),
                pltpu.SemaphoreType.DMA((ITERS, peers - 1)),
                pltpu.SemaphoreType.DMA((len(operands),)),
            ],
            compiler_params=pltpu.CompilerParams(
                collective_id=0, has_side_effects=True, vmem_limit_bytes=24 * 1024 * 1024
            ),
        )(*(x if x.size == 1 else pltpu.with_memory_space_constraint(x, pltpu.HBM) for x in operands))
        return jnp.swapaxes(trace_field, 1, 2), jnp.swapaxes(robin_data, 1, 2), coefficients

    in_specs = (
        P("grp", "sub", None, None),
        P("grp", "sub", None, None, None, None),
        P("grp", "sub", None, None),
        P("grp", "sub"),
        P("grp", "sub", None, None),
        P("grp", "sub", None),
        P("grp", "sub", None, None, None),
        P("grp", "sub", None, None),
        P("grp", "sub", None, None, None),
        P("grp", "sub", None),
    )
    out_specs = (P("grp", "sub", None, None), P("grp", "sub", None, None), P("grp", "sub", None))
    return jax.shard_map(body, mesh=mesh, in_specs=in_specs, out_specs=out_specs, check_vma=False)
```

```python
import functools

import jax
import jax.numpy as jnp
from jax import lax
from jax.experimental import pallas as pl
from jax.experimental.pallas import tpu as pltpu
from jax.sharding import PartitionSpec as P

ITERS = 3
SWEEPS = 2
CSWEEPS = 2
LANES = 128

robin_weight = 1.0
omega_step = 0.2
highest = lax.Precision.HIGHEST
MESH = pl.DeviceIdType.MESH


def pick_lanes(field, index):
    rows = field.shape[0]
    parts = []
    for d in range(index.shape[1] // LANES):
        wanted = jnp.broadcast_to(index[:, d * LANES : (d + 1) * LANES], (rows, LANES))
        within = wanted & (LANES - 1)
        chunk = wanted >> (LANES.bit_length() - 1)
        out = None
        for s in range(field.shape[1] // LANES):
            got = jnp.take_along_axis(
                field[:, s * LANES : (s + 1) * LANES], within, axis=1, mode="promise_in_bounds"
            )
            out = got if out is None else jnp.where(chunk == s, got, out)
        parts.append(out)
    return jnp.concatenate(parts, axis=1) if len(parts) > 1 else parts[0]


def iota(shape, dim):
    return lax.broadcasted_iota(jnp.int32, shape, dim)


def kernel(
    groups,
    peers,
    load_hbm,
    couple_hbm,
    link_hbm,
    count_hbm,
    slot_hbm,
    pair_hbm,
    basis_hbm,
    inverse_hbm,
    block_hbm,
    coarse_link_hbm,
    trace_out,
    robin_out,
    coef_out,
    load_ref,
    couple_ref,
    link_ref,
    count_ref,
    slot_ref,
    pair_ref,
    basis_ref,
    inverse_ref,
    block_ref,
    coarse_link_ref,
    load_s,
    trace_s,
    robin_s,
    stack_s,
    couple_s,
    moved_s,
    table_s,
    folded_s,
    slots_s,
    inside_s,
    owner_s,
    interface_s,
    start_s,
    coef_s,
    coarse_send,
    coarse_recv,
    robin_send,
    robin_recv,
    coarse_send_sem,
    coarse_recv_sem,
    robin_send_sem,
    robin_recv_sem,
    input_sem,
):
    g, me = lax.axis_index("grp"), lax.axis_index("sub")
    trace_dim, faces = load_ref.shape[1], load_ref.shape[-1]
    rows = load_s.shape[0]
    cvec = inverse_ref.shape[-1]
    links = link_ref.shape[1]
    kc = coarse_link_ref.shape[-1]
    cap = slot_ref.shape[-1]
    slot_lanes = peers * cap

    def per_group(act):
        @pl.when(g > 0)
        def _():
            act(-1)

        @pl.when(g < groups - 1)
        def _():
            act(1)

        act(0)

    def after(off):
        return jnp.where(me + off >= peers, me + off - peers, me + off)

    def targets(d):
        first = 1 if d == 0 else 0
        offsets = sorted(range(first, peers), key=lambda off: -min(off, peers - off))
        return [(g + d, after(off)) for off in offsets]

    def far_first(act):
        even = lax.rem(g, 2) == 0
        pl.when(even & (g > 0))(lambda: act(-1))
        pl.when(g < groups - 1)(lambda: act(1))
        pl.when(jnp.logical_not(even))(lambda: act(-1))
        act(0)

    operands = (
        (count_hbm, count_ref),
        (load_hbm, load_ref),
        (link_hbm, link_ref),
        (slot_hbm, slot_ref),
        (pair_hbm, pair_ref),
        (couple_hbm, couple_ref),
        (inverse_hbm, inverse_ref),
        (basis_hbm, basis_ref),
        (block_hbm, block_ref),
        (coarse_link_hbm, coarse_link_ref),
    )
    fetches = [
        pltpu.make_async_copy(src, dst, input_sem.at[i]) for i, (src, dst) in enumerate(operands)
    ]
    for fetch in fetches:
        fetch.start()
    barrier = pltpu.get_barrier_semaphore()

    def greet(d):
        for device in targets(d):
            pl.semaphore_signal(barrier, inc=1, device_id=device, device_id_type=MESH)

    per_group(greet)

    for fetch in fetches[:5]:
        fetch.wait()
    live = (iota((1, faces), 1) < count_ref[0, 0]).astype(jnp.float32)
    load_s[...] = jnp.zeros_like(load_s)
    for a in range(trace_dim):
        load_s[a : a + 1, :] = load_ref[0, a] * live
    moved_s[...] = jnp.zeros_like(moved_s)

    def unpack(b, carry):
        for s in range(faces // LANES):
            for k in range(links + 1):
                couple_s[s, b, (k + 1) * rows - 8 : (k + 1) * rows, :] = jnp.zeros((8, LANES), jnp.float32)
        for a in range(trace_dim):
            blocks = couple_ref[0, 0, a, b].astype(jnp.float32)
            for s in range(faces // LANES):
                couple_s[s, b, pl.ds(a, links + 1, stride=rows), :] = blocks[:, s * LANES : (s + 1) * LANES]
        return carry

    coarse_send[...] = jnp.zeros_like(coarse_send)
    slots_s[...] = jnp.zeros_like(slots_s)
    inside = jnp.zeros((1, faces), jnp.float32)
    owner = jnp.full((1, faces), -1.0, jnp.float32)
    eye_slots = iota((cap, cap), 0) == iota((cap, cap), 1)
    face_ids = iota((cap, faces), 1).astype(jnp.float32)
    place = iota((cap, faces), 0)
    for j in range(peers):
        slot_row = slot_ref[0, 0, j : j + 1, :]
        slots_s[:, j * cap : (j + 1) * cap] = slot_row
        as_float = jnp.broadcast_to(slot_row.astype(jnp.float32), (cap, cap))
        column = jnp.sum(jnp.where(eye_slots, as_float, 0.0), axis=1, keepdims=True)
        hit = (column == face_ids) & (place < pair_ref[0, 0, j])
        found = jnp.max(jnp.where(hit, place.astype(jnp.float32), -1.0), axis=0, keepdims=True)
        inside = jnp.where(found >= 0.0, found, inside)
        owner = jnp.where(found >= 0.0, float(j), owner)
    interface_s[...] = jnp.where(owner >= 0.0, 1.0, 0.0)
    inside_s[...] = inside.astype(jnp.int32)
    owner_s[...] = owner.astype(jnp.int32)
    robin_s[...] = jnp.zeros_like(robin_s)
    trace_s[...] = omega_step * load_s[...]
    eye = iota((cvec, cvec), 0) == iota((cvec, cvec), 1)

    fetches[5].wait()
    lax.fori_loop(0, trace_dim, unpack, 0)
    count = (peers - 1) + jnp.where(g > 0, peers, 0) + jnp.where(g < groups - 1, peers, 0)

    def apply(x):
        stack_s[0] = x
        for k in range(links):
            stack_s[k + 1] = pick_lanes(x, link_ref[0, k])
        chunks = []
        for s in range(faces // LANES):
            lanes = slice(s * LANES, (s + 1) * LANES)
            totals = []
            for k in range(links + 1):
                total = None
                for b in range(trace_dim):
                    term = couple_s[s, b, k * rows : (k + 1) * rows, :] * stack_s[k, b : b + 1, lanes]
                    total = term if total is None else total + term
                totals.append(total)
            chunks.append(functools.reduce(jnp.add, totals))
        product = jnp.concatenate(chunks, axis=1)
        return live * (product + robin_weight * interface_s[...] * x)

    def right_side():
        return load_s[...] + live * robin_s[...]

    def sweep(x, bx):
        return x + omega_step * (right_side() - bx)

    def as_row(column):
        return jnp.sum(jnp.where(eye, column, 0.0), axis=0, keepdims=True)

    def send_row(t, r, row):
        coarse_send[t, r, :, 0:cvec] = row

        def push(d):
            for device in targets(d):
                pltpu.make_async_remote_copy(
                    src_ref=coarse_send.at[t, r],
                    dst_ref=coarse_recv.at[t, r, (1 - d) * peers + me],
                    send_sem=coarse_send_sem.at[t, r, 1 + d],
                    recv_sem=coarse_recv_sem.at[t, r, 1 - d],
                    device_id=device,
                    device_id_type=MESH,
                ).start()

        far_first(push)

    def wait_rows(t, r, sems):
        def wait(d):
            n = peers - 1 if d == 0 else peers
            part = coarse_recv.at[t, r, pl.ds((1 + d) * peers, n)]
            pltpu.make_async_copy(part, part, sems.at[t, r, 1 + d]).wait()

        per_group(wait)

    def coupled(t, r):
        table_s[...] = coarse_recv[t, r]
        total = None
        for k in range(kc):
            position = coarse_link_ref[0, 0, k] - (g - 1) * peers
            position = jnp.minimum(jnp.maximum(position, 0), 3 * peers - 1)
            term = folded_s[k] * table_s[position][:, 0:cvec]
            total = term if total is None else total + term
        return jnp.sum(total, axis=1, keepdims=True)

    def robin_copy(t, off):
        to = after(off)
        chunk = lax.div(to * cap, LANES)
        return pltpu.make_async_remote_copy(
            src_ref=robin_send.at[t, chunk],
            dst_ref=robin_recv.at[t, off - 1],
            send_sem=robin_send_sem.at[t, off - 1],
            recv_sem=robin_recv_sem.at[t, off - 1],
            device_id=(g, to),
            device_id_type=MESH,
        )

    def fold():
        for k in range(kc):
            folded_s[k] = jnp.dot(
                inverse_ref[0, 0],
                block_ref[0, 0, k],
                precision=highest,
                preferred_element_type=jnp.float32,
            )

    def relax(bx):
        trace_s[...] = sweep(trace_s[...], bx)

    def coarse(t, bx):
        residual = right_side() - bx
        part = jnp.zeros((cvec, LANES), jnp.float32)
        for a in range(trace_dim):
            product = basis_ref[0, 0, a] * residual[a : a + 1, :]
            for s in range(faces // LANES):
                part = part + product[:, s * LANES : (s + 1) * LANES]
        restricted = jnp.sum(part, axis=1, keepdims=True)
        start = jnp.sum(inverse_ref[0, 0] * as_row(restricted), axis=1, keepdims=True)
        start_s[...] = jnp.broadcast_to(start, start_s.shape)
        coef_s[...] = start_s[...]

        def exchange(r, carry):
            send_row(t, r, as_row(coef_s[:, 0:cvec]))
            pl.when((t == 0) & (r == 0))(fold)
            wait_rows(t, r, coarse_recv_sem)
            coef_s[...] = start_s[...] - coupled(t, r)
            return carry

        lax.fori_loop(0, CSWEEPS, exchange, 0)
        coef_out[0] = as_row(coef_s[:, 0:cvec])
        wide = jnp.concatenate([coef_s[...]] * (faces // LANES), axis=1)
        for a in range(trace_dim):
            moved_s[a : a + 1, :] = jnp.sum(basis_ref[0, 0, a] * wide, axis=0, keepdims=True)
        x = trace_s[...] + live * moved_s[...]
        trace_s[...] = x
        outgoing = 2.0 * robin_weight * x - robin_s[...]
        sent = pick_lanes(outgoing, slots_s[...])
        for s in range(slots_s.shape[1] // LANES):
            robin_send[t, s] = sent[:, s * LANES : (s + 1) * LANES]
        for off in range(1, peers):
            robin_copy(t, off).start()
        for a in range(trace_dim):
            trace_out[0, a] = x[a : a + 1, :]

    def settle(t, bx):
        base = lax.rem(me * cap, LANES)
        inside = inside_s[...] + base
        owner = owner_s[...]
        fresh = jnp.zeros((rows, faces), jnp.float32)
        for off in range(1, peers):
            robin_copy(t, off).wait_recv()
            source = after(peers - off)
            got = pick_lanes(robin_recv[t, off - 1], inside)
            fresh = jnp.where(owner == source, got, fresh)
        robin_s[...] = fresh
        trace_s[...] = sweep(trace_s[...], bx)
        for r in range(CSWEEPS):
            wait_rows(t, r, coarse_send_sem)
        for off in range(1, peers):
            robin_copy(t, off).wait_send()

    phases = SWEEPS + 1

    def step(n, carry):
        t = n // phases
        phase = n - t * phases
        bx = apply(trace_s[...])
        pl.when(phase < SWEEPS - 1)(lambda: relax(bx))

        @pl.when(n == SWEEPS - 1)
        def _():
            pl.semaphore_wait(barrier, count)
            for fetch in fetches[6:]:
                fetch.wait()

        pl.when(phase == SWEEPS - 1)(lambda: coarse(t, bx))
        pl.when(phase == SWEEPS)(lambda: settle(t, bx))
        return carry

    lax.fori_loop(0, ITERS * phases, step, 0)
    for a in range(trace_dim):
        robin_out[0, a] = robin_s[a : a + 1, :]


def solution(mesh):
    groups, peers = mesh.shape["grp"], mesh.shape["sub"]

    def body(
        load,
        couple,
        face_link,
        face_count,
        slot_face,
        pair_count,
        basis,
        coarse_inverse,
        coarse_block,
        coarse_link,
    ):
        trace_dim, faces = load.shape[-2:]
        rows = -(-trace_dim // 8) * 8
        links = face_link.shape[-2]
        cvec = basis.shape[2]
        kc = coarse_link.shape[-1]
        cap = slot_face.shape[-1]
        chunks = -(-peers * cap // LANES)
        vmem, smem = pltpu.VMEM, pltpu.SMEM
        operands = (
            jnp.swapaxes(load, 1, 2),
            jnp.transpose(couple, (0, 1, 3, 4, 2, 5)),
            jnp.swapaxes(face_link, 1, 2),
            face_count,
            slot_face,
            pair_count,
            jnp.swapaxes(basis, 2, 3),
            coarse_inverse,
            coarse_block,
            coarse_link,
        )
        f32 = jnp.float32
        spec = lambda space: pl.BlockSpec(memory_space=space)
        trace_field, robin_data, coefficients = pl.pallas_call(
            functools.partial(kernel, groups, peers),
            out_shape=(
                jax.ShapeDtypeStruct((1, trace_dim, 1, faces), f32),
                jax.ShapeDtypeStruct((1, trace_dim, 1, faces), f32),
                jax.ShapeDtypeStruct((1, 1, cvec), f32),
            ),
            in_specs=[spec(pl.ANY)] * len(operands),
            out_specs=(spec(vmem), spec(vmem), spec(vmem)),
            scratch_shapes=[
                space(x.shape, x.dtype)
                for x, space in zip(operands, (vmem, vmem, vmem, smem, vmem, smem, vmem, vmem, vmem, smem))
            ]
            + [
                vmem((rows, faces), f32),
                vmem((rows, faces), f32),
                vmem((rows, faces), f32),
                vmem((links + 1, rows, faces), f32),
                vmem((faces // LANES, trace_dim, (links + 1) * rows, LANES), f32),
                vmem((rows, faces), f32),
                vmem((3 * peers, 1, LANES), f32),
                vmem((kc, cvec, cvec), f32),
                vmem((1, chunks * LANES), jnp.int32),
                vmem((1, faces), jnp.int32),
                vmem((1, faces), jnp.int32),
                vmem((1, faces), f32),
                vmem((cvec, LANES), f32),
                vmem((cvec, LANES), f32),
                vmem((ITERS, CSWEEPS, 1, LANES), f32),
                vmem((ITERS, CSWEEPS, 3 * peers, 1, LANES), f32),
                vmem((ITERS, chunks, rows, LANES), f32),
                vmem((ITERS, peers - 1, rows, LANES), f32),
                pltpu.SemaphoreType.DMA((ITERS, CSWEEPS, 3)),
                pltpu.SemaphoreType.DMA((ITERS, CSWEEPS, 3)),
                pltpu.SemaphoreType.DMA((ITERS, peers - 1)),
                pltpu.SemaphoreType.DMA((ITERS, peers - 1)),
                pltpu.SemaphoreType.DMA((len(operands),)),
            ],
            compiler_params=pltpu.CompilerParams(
                collective_id=0, has_side_effects=True, vmem_limit_bytes=24 * 1024 * 1024
            ),
        )(*(x if x.size == 1 else pltpu.with_memory_space_constraint(x, pltpu.HBM) for x in operands))
        return jnp.swapaxes(trace_field, 1, 2), jnp.swapaxes(robin_data, 1, 2), coefficients

    in_specs = (
        P("grp", "sub", None, None),
        P("grp", "sub", None, None, None, None),
        P("grp", "sub", None, None),
        P("grp", "sub"),
        P("grp", "sub", None, None),
        P("grp", "sub", None),
        P("grp", "sub", None, None, None),
        P("grp", "sub", None, None),
        P("grp", "sub", None, None, None),
        P("grp", "sub", None),
    )
    out_specs = (P("grp", "sub", None, None), P("grp", "sub", None, None), P("grp", "sub", None))
    return jax.shard_map(body, mesh=mesh, in_specs=in_specs, out_specs=out_specs, check_vma=False)
```

```python
import functools

import jax
import jax.numpy as jnp
from jax import lax
from jax.experimental import pallas as pl
from jax.experimental.pallas import tpu as pltpu
from jax.sharding import PartitionSpec as P

ITERS = 3
SWEEPS = 2
CSWEEPS = 2
LANES = 128

robin_weight = 1.0
omega_step = 0.2
highest = lax.Precision.HIGHEST
MESH = pl.DeviceIdType.MESH


def pick_lanes(field, index):
    rows = field.shape[0]
    parts = []
    for d in range(index.shape[1] // LANES):
        wanted = jnp.broadcast_to(index[:, d * LANES : (d + 1) * LANES], (rows, LANES))
        within = wanted & (LANES - 1)
        chunk = wanted >> (LANES.bit_length() - 1)
        out = None
        for s in range(field.shape[1] // LANES):
            got = jnp.take_along_axis(
                field[:, s * LANES : (s + 1) * LANES], within, axis=1, mode="promise_in_bounds"
            )
            out = got if out is None else jnp.where(chunk == s, got, out)
        parts.append(out)
    return jnp.concatenate(parts, axis=1) if len(parts) > 1 else parts[0]


def iota(shape, dim):
    return lax.broadcasted_iota(jnp.int32, shape, dim)


def kernel(
    groups,
    peers,
    load_hbm,
    couple_hbm,
    link_hbm,
    count_hbm,
    slot_hbm,
    pair_hbm,
    basis_hbm,
    inverse_hbm,
    block_hbm,
    coarse_link_hbm,
    trace_out,
    robin_out,
    coef_out,
    load_ref,
    couple_ref,
    link_ref,
    count_ref,
    slot_ref,
    pair_ref,
    basis_ref,
    inverse_ref,
    block_ref,
    coarse_link_ref,
    load_s,
    trace_s,
    robin_s,
    stack_s,
    couple_s,
    moved_s,
    table_s,
    folded_s,
    shared_s,
    slots_s,
    inside_s,
    owner_s,
    interface_s,
    start_s,
    coef_s,
    coarse_send,
    coarse_recv,
    robin_send,
    robin_recv,
    coarse_send_sem,
    coarse_recv_sem,
    robin_send_sem,
    robin_recv_sem,
    input_sem,
):
    g, me = lax.axis_index("grp"), lax.axis_index("sub")
    trace_dim, faces = load_ref.shape[1], load_ref.shape[-1]
    rows = load_s.shape[0]
    cvec = inverse_ref.shape[-1]
    links = link_ref.shape[1]
    kc = coarse_link_ref.shape[-1]
    cap = slot_ref.shape[-1]
    slot_lanes = peers * cap

    def per_group(act):
        @pl.when(g > 0)
        def _():
            act(-1)

        @pl.when(g < groups - 1)
        def _():
            act(1)

        act(0)

    def after(off):
        return jnp.where(me + off >= peers, me + off - peers, me + off)

    def targets(d):
        first = 1 if d == 0 else 0
        offsets = sorted(range(first, peers), key=lambda off: -min(off, peers - off))
        return [(g + d, after(off)) for off in offsets]

    def far_first(act):
        even = lax.rem(g, 2) == 0
        pl.when(even & (g > 0))(lambda: act(-1))
        pl.when(g < groups - 1)(lambda: act(1))
        pl.when(jnp.logical_not(even))(lambda: act(-1))
        act(0)

    operands = (
        (count_hbm, count_ref),
        (load_hbm, load_ref),
        (link_hbm, link_ref),
        (slot_hbm, slot_ref),
        (pair_hbm, pair_ref),
        (couple_hbm, couple_ref),
        (inverse_hbm, inverse_ref),
        (basis_hbm, basis_ref),
        (block_hbm, block_ref),
        (coarse_link_hbm, coarse_link_ref),
    )
    fetches = [
        pltpu.make_async_copy(src, dst, input_sem.at[i]) for i, (src, dst) in enumerate(operands)
    ]
    for fetch in fetches:
        fetch.start()
    barrier = pltpu.get_barrier_semaphore()

    def greet(d):
        for device in targets(d):
            pl.semaphore_signal(barrier, inc=1, device_id=device, device_id_type=MESH)

    per_group(greet)

    for fetch in fetches[:5]:
        fetch.wait()
    live = (iota((1, faces), 1) < count_ref[0, 0]).astype(jnp.float32)
    load_s[...] = jnp.zeros_like(load_s)
    for a in range(trace_dim):
        load_s[a : a + 1, :] = load_ref[0, a] * live
    moved_s[...] = jnp.zeros_like(moved_s)

    def unpack(b, carry):
        for s in range(faces // LANES):
            for k in range(links + 1):
                couple_s[s, b, (k + 1) * rows - 8 : (k + 1) * rows, :] = jnp.zeros((8, LANES), jnp.float32)
        for a in range(trace_dim):
            blocks = couple_ref[0, 0, a, b].astype(jnp.float32)
            for s in range(faces // LANES):
                couple_s[s, b, pl.ds(a, links + 1, stride=rows), :] = blocks[:, s * LANES : (s + 1) * LANES]
        return carry

    coarse_send[...] = jnp.zeros_like(coarse_send)
    slots_s[...] = jnp.zeros_like(slots_s)
    inside = jnp.zeros((1, faces), jnp.float32)
    owner = jnp.full((1, faces), -1.0, jnp.float32)
    eye_slots = iota((cap, cap), 0) == iota((cap, cap), 1)
    face_ids = iota((cap, faces), 1).astype(jnp.float32)
    place = iota((cap, faces), 0)
    for j in range(peers):
        slot_row = slot_ref[0, 0, j : j + 1, :]
        slots_s[:, j * cap : (j + 1) * cap] = slot_row
        as_float = jnp.broadcast_to(slot_row.astype(jnp.float32), (cap, cap))
        column = jnp.sum(jnp.where(eye_slots, as_float, 0.0), axis=1, keepdims=True)
        hit = (column == face_ids) & (place < pair_ref[0, 0, j])
        found = jnp.max(jnp.where(hit, place.astype(jnp.float32), -1.0), axis=0, keepdims=True)
        inside = jnp.where(found >= 0.0, found, inside)
        owner = jnp.where(found >= 0.0, float(j), owner)
    interface_s[...] = jnp.where(owner >= 0.0, 1.0, 0.0)
    inside_s[...] = inside.astype(jnp.int32)
    owner_s[...] = owner.astype(jnp.int32)
    robin_s[...] = jnp.zeros_like(robin_s)
    trace_s[...] = omega_step * load_s[...]
    eye = iota((cvec, cvec), 0) == iota((cvec, cvec), 1)

    fetches[5].wait()
    lax.fori_loop(0, trace_dim, unpack, 0, unroll=3)
    count = (peers - 1) + jnp.where(g > 0, peers, 0) + jnp.where(g < groups - 1, peers, 0)

    def apply(x):
        stack_s[0] = x
        for k in range(links):
            stack_s[k + 1] = pick_lanes(x, link_ref[0, k])
        chunks = []
        for s in range(faces // LANES):
            lanes = slice(s * LANES, (s + 1) * LANES)
            totals = []
            for k in range(links + 1):
                total = None
                for b in range(trace_dim):
                    term = couple_s[s, b, k * rows : (k + 1) * rows, :] * stack_s[k, b : b + 1, lanes]
                    total = term if total is None else total + term
                totals.append(total)
            chunks.append(functools.reduce(jnp.add, totals))
        product = jnp.concatenate(chunks, axis=1)
        return live * (product + robin_weight * interface_s[...] * x)

    def right_side():
        return load_s[...] + live * robin_s[...]

    def sweep(x, bx):
        return x + omega_step * (right_side() - bx)

    def as_row(column):
        return jnp.sum(jnp.where(eye, column, 0.0), axis=0, keepdims=True)

    def send_row(t, r, row):
        coarse_send[t, r, :, 0:cvec] = row

        def push(d):
            for device in targets(d):
                pltpu.make_async_remote_copy(
                    src_ref=coarse_send.at[t, r],
                    dst_ref=coarse_recv.at[t, r, (1 - d) * peers + me],
                    send_sem=coarse_send_sem.at[t, r, 1 + d],
                    recv_sem=coarse_recv_sem.at[t, r, 1 - d],
                    device_id=device,
                    device_id_type=MESH,
                ).start()

        far_first(push)

    def wait_rows(t, r, sems):
        def wait(d):
            n = peers - 1 if d == 0 else peers
            part = coarse_recv.at[t, r, pl.ds((1 + d) * peers, n)]
            pltpu.make_async_copy(part, part, sems.at[t, r, 1 + d]).wait()

        per_group(wait)

    def coupled(t, r):
        table_s[...] = coarse_recv[t, r]
        total = None
        for k in range(kc):
            position = coarse_link_ref[0, 0, k] - (g - 1) * peers
            position = jnp.minimum(jnp.maximum(position, 0), 3 * peers - 1)
            term = folded_s[k] * table_s[position][:, 0:cvec]
            total = term if total is None else total + term
        return jnp.sum(total, axis=1, keepdims=True)

    def robin_copy(t, off):
        to = after(off)
        chunk = lax.div(to * cap, LANES)
        return pltpu.make_async_remote_copy(
            src_ref=robin_send.at[t, chunk],
            dst_ref=robin_recv.at[t, off - 1],
            send_sem=robin_send_sem.at[t, off - 1],
            recv_sem=robin_recv_sem.at[t, off - 1],
            device_id=(g, to),
            device_id_type=MESH,
        )

    def fold():
        for a in range(trace_dim):
            shared = pick_lanes(basis_ref[0, 0, a], slots_s[...])
            for s in range(slots_s.shape[1] // LANES):
                shared_s[s, a] = shared[:, s * LANES : (s + 1) * LANES]
        for k in range(kc):
            folded_s[k] = jnp.dot(
                inverse_ref[0, 0],
                block_ref[0, 0, k],
                precision=highest,
                preferred_element_type=jnp.float32,
            )

    def relax(bx):
        trace_s[...] = sweep(trace_s[...], bx)

    def prepare(t):
        outgoing = 2.0 * robin_weight * trace_s[...] - robin_s[...]
        sent = pick_lanes(outgoing, slots_s[...])
        for s in range(slots_s.shape[1] // LANES):
            robin_send[t, s] = sent[:, s * LANES : (s + 1) * LANES]

    def coarse(t, bx):
        residual = right_side() - bx
        part = jnp.zeros((cvec, LANES), jnp.float32)
        for a in range(trace_dim):
            product = basis_ref[0, 0, a] * residual[a : a + 1, :]
            for s in range(faces // LANES):
                part = part + product[:, s * LANES : (s + 1) * LANES]
        restricted = jnp.sum(part, axis=1, keepdims=True)
        start = jnp.sum(inverse_ref[0, 0] * as_row(restricted), axis=1, keepdims=True)
        start_s[...] = jnp.broadcast_to(start, start_s.shape)
        coef_s[...] = start_s[...]

        def exchange(r, carry):
            send_row(t, r, as_row(coef_s[:, 0:cvec]))
            pl.when((t == 0) & (r == 0))(fold)
            pl.when(r == 0)(lambda: prepare(t))
            wait_rows(t, r, coarse_recv_sem)
            coef_s[...] = start_s[...] - coupled(t, r)
            return carry

        lax.fori_loop(0, CSWEEPS, exchange, 0)
        for s in range(slots_s.shape[1] // LANES):
            for a in range(trace_dim):
                moved = jnp.sum(shared_s[s, a] * coef_s[...], axis=0, keepdims=True)
                robin_send[t, s, a : a + 1, :] += 2.0 * robin_weight * moved
        for off in range(1, peers):
            robin_copy(t, off).start()
        coef_out[0] = as_row(coef_s[:, 0:cvec])
        wide = jnp.concatenate([coef_s[...]] * (faces // LANES), axis=1)
        for a in range(trace_dim):
            moved_s[a : a + 1, :] = jnp.sum(basis_ref[0, 0, a] * wide, axis=0, keepdims=True)
        x = trace_s[...] + live * moved_s[...]
        trace_s[...] = x
        for a in range(trace_dim):
            trace_out[0, a] = x[a : a + 1, :]

    def settle(t, bx):
        base = lax.rem(me * cap, LANES)
        inside = inside_s[...] + base
        owner = owner_s[...]
        fresh = jnp.zeros((rows, faces), jnp.float32)
        for off in range(1, peers):
            robin_copy(t, off).wait_recv()
            source = after(peers - off)
            got = pick_lanes(robin_recv[t, off - 1], inside)
            fresh = jnp.where(owner == source, got, fresh)
        robin_s[...] = fresh
        trace_s[...] = sweep(trace_s[...], bx)
        for r in range(CSWEEPS):
            wait_rows(t, r, coarse_send_sem)
        for off in range(1, peers):
            robin_copy(t, off).wait_send()

    phases = SWEEPS + 1

    def step(n, carry):
        t = n // phases
        phase = n - t * phases
        bx = apply(trace_s[...])
        pl.when(phase < SWEEPS - 1)(lambda: relax(bx))

        @pl.when(n == SWEEPS - 1)
        def _():
            pl.semaphore_wait(barrier, count)
            for fetch in fetches[6:]:
                fetch.wait()

        pl.when(phase == SWEEPS - 1)(lambda: coarse(t, bx))
        pl.when(phase == SWEEPS)(lambda: settle(t, bx))
        return carry

    lax.fori_loop(0, ITERS * phases, step, 0)
    for a in range(trace_dim):
        robin_out[0, a] = robin_s[a : a + 1, :]


def solution(mesh):
    groups, peers = mesh.shape["grp"], mesh.shape["sub"]

    def body(
        load,
        couple,
        face_link,
        face_count,
        slot_face,
        pair_count,
        basis,
        coarse_inverse,
        coarse_block,
        coarse_link,
    ):
        trace_dim, faces = load.shape[-2:]
        rows = -(-trace_dim // 8) * 8
        links = face_link.shape[-2]
        cvec = basis.shape[2]
        kc = coarse_link.shape[-1]
        cap = slot_face.shape[-1]
        chunks = -(-peers * cap // LANES)
        vmem, smem = pltpu.VMEM, pltpu.SMEM
        operands = (
            jnp.swapaxes(load, 1, 2),
            jnp.transpose(couple, (0, 1, 3, 4, 2, 5)),
            jnp.swapaxes(face_link, 1, 2),
            face_count,
            slot_face,
            pair_count,
            jnp.swapaxes(basis, 2, 3),
            coarse_inverse,
            coarse_block,
            coarse_link,
        )
        f32 = jnp.float32
        spec = lambda space: pl.BlockSpec(memory_space=space)
        trace_field, robin_data, coefficients = pl.pallas_call(
            functools.partial(kernel, groups, peers),
            out_shape=(
                jax.ShapeDtypeStruct((1, trace_dim, 1, faces), f32),
                jax.ShapeDtypeStruct((1, trace_dim, 1, faces), f32),
                jax.ShapeDtypeStruct((1, 1, cvec), f32),
            ),
            in_specs=[spec(pl.ANY)] * len(operands),
            out_specs=(spec(vmem), spec(vmem), spec(vmem)),
            scratch_shapes=[
                space(x.shape, x.dtype)
                for x, space in zip(operands, (vmem, vmem, vmem, smem, vmem, smem, vmem, vmem, vmem, smem))
            ]
            + [
                vmem((rows, faces), f32),
                vmem((rows, faces), f32),
                vmem((rows, faces), f32),
                vmem((links + 1, rows, faces), f32),
                vmem((faces // LANES, trace_dim, (links + 1) * rows, LANES), f32),
                vmem((rows, faces), f32),
                vmem((3 * peers, 1, LANES), f32),
                vmem((kc, cvec, cvec), f32),
                vmem((chunks, trace_dim, cvec, LANES), f32),
                vmem((1, chunks * LANES), jnp.int32),
                vmem((1, faces), jnp.int32),
                vmem((1, faces), jnp.int32),
                vmem((1, faces), f32),
                vmem((cvec, LANES), f32),
                vmem((cvec, LANES), f32),
                vmem((ITERS, CSWEEPS, 1, LANES), f32),
                vmem((ITERS, CSWEEPS, 3 * peers, 1, LANES), f32),
                vmem((ITERS, chunks, rows, LANES), f32),
                vmem((ITERS, peers - 1, rows, LANES), f32),
                pltpu.SemaphoreType.DMA((ITERS, CSWEEPS, 3)),
                pltpu.SemaphoreType.DMA((ITERS, CSWEEPS, 3)),
                pltpu.SemaphoreType.DMA((ITERS, peers - 1)),
                pltpu.SemaphoreType.DMA((ITERS, peers - 1)),
                pltpu.SemaphoreType.DMA((len(operands),)),
            ],
            compiler_params=pltpu.CompilerParams(
                collective_id=0, has_side_effects=True, vmem_limit_bytes=24 * 1024 * 1024
            ),
        )(*(x if x.size == 1 else pltpu.with_memory_space_constraint(x, pltpu.HBM) for x in operands))
        return jnp.swapaxes(trace_field, 1, 2), jnp.swapaxes(robin_data, 1, 2), coefficients

    in_specs = (
        P("grp", "sub", None, None),
        P("grp", "sub", None, None, None, None),
        P("grp", "sub", None, None),
        P("grp", "sub"),
        P("grp", "sub", None, None),
        P("grp", "sub", None),
        P("grp", "sub", None, None, None),
        P("grp", "sub", None, None),
        P("grp", "sub", None, None, None),
        P("grp", "sub", None),
    )
    out_specs = (P("grp", "sub", None, None), P("grp", "sub", None, None), P("grp", "sub", None))
    return jax.shard_map(body, mesh=mesh, in_specs=in_specs, out_specs=out_specs, check_vma=False)
```

```python
import functools

import jax
import jax.numpy as jnp
from jax import lax
from jax.experimental import pallas as pl
from jax.experimental.pallas import tpu as pltpu
from jax.sharding import PartitionSpec as P

ITERS = 3
SWEEPS = 2
CSWEEPS = 2
LANES = 128

robin_weight = 1.0
omega_step = 0.2
highest = lax.Precision.HIGHEST
MESH = pl.DeviceIdType.MESH


def pick_lanes(field, index):
    rows = field.shape[0]
    parts = []
    for d in range(index.shape[1] // LANES):
        wanted = jnp.broadcast_to(index[:, d * LANES : (d + 1) * LANES], (rows, LANES))
        within = wanted & (LANES - 1)
        chunk = wanted >> (LANES.bit_length() - 1)
        out = None
        for s in range(field.shape[1] // LANES):
            got = jnp.take_along_axis(
                field[:, s * LANES : (s + 1) * LANES], within, axis=1, mode="promise_in_bounds"
            )
            out = got if out is None else jnp.where(chunk == s, got, out)
        parts.append(out)
    return jnp.concatenate(parts, axis=1) if len(parts) > 1 else parts[0]


def iota(shape, dim):
    return lax.broadcasted_iota(jnp.int32, shape, dim)


def kernel(
    groups,
    peers,
    load_hbm,
    couple_hbm,
    link_hbm,
    count_hbm,
    slot_hbm,
    pair_hbm,
    basis_hbm,
    inverse_hbm,
    block_hbm,
    coarse_link_hbm,
    trace_out,
    robin_out,
    coef_out,
    load_ref,
    couple_ref,
    link_ref,
    count_ref,
    slot_ref,
    pair_ref,
    basis_ref,
    inverse_ref,
    block_ref,
    coarse_link_ref,
    load_s,
    trace_s,
    robin_s,
    stack_s,
    couple_s,
    moved_s,
    table_s,
    folded_s,
    shared_s,
    slots_s,
    inside_s,
    owner_s,
    interface_s,
    coef_s,
    coarse_send,
    coarse_recv,
    robin_send,
    robin_recv,
    coarse_send_sem,
    coarse_recv_sem,
    robin_send_sem,
    robin_recv_sem,
    input_sem,
):
    g, me = lax.axis_index("grp"), lax.axis_index("sub")
    trace_dim, faces = load_ref.shape[1], load_ref.shape[-1]
    rows = load_s.shape[0]
    cvec = inverse_ref.shape[-1]
    links = link_ref.shape[1]
    kc = coarse_link_ref.shape[-1]
    cap = slot_ref.shape[-1]
    slot_lanes = peers * cap

    def per_group(act):
        @pl.when(g > 0)
        def _():
            act(-1)

        @pl.when(g < groups - 1)
        def _():
            act(1)

        act(0)

    def after(off):
        return jnp.where(me + off >= peers, me + off - peers, me + off)

    def targets(d):
        first = 1 if d == 0 else 0
        offsets = sorted(range(first, peers), key=lambda off: -min(off, peers - off))
        return [(g + d, after(off)) for off in offsets]

    def far_first(act):
        even = lax.rem(g, 2) == 0
        pl.when(even & (g > 0))(lambda: act(-1))
        pl.when(g < groups - 1)(lambda: act(1))
        pl.when(jnp.logical_not(even))(lambda: act(-1))
        act(0)

    operands = (
        (count_hbm, count_ref),
        (load_hbm, load_ref),
        (link_hbm, link_ref),
        (slot_hbm, slot_ref),
        (pair_hbm, pair_ref),
        (couple_hbm, couple_ref),
        (inverse_hbm, inverse_ref),
        (basis_hbm, basis_ref),
        (block_hbm, block_ref),
        (coarse_link_hbm, coarse_link_ref),
    )
    fetches = [
        pltpu.make_async_copy(src, dst, input_sem.at[i]) for i, (src, dst) in enumerate(operands)
    ]
    for fetch in fetches:
        fetch.start()
    barrier = pltpu.get_barrier_semaphore()

    def greet(d):
        for device in targets(d):
            pl.semaphore_signal(barrier, inc=1, device_id=device, device_id_type=MESH)

    per_group(greet)

    for fetch in fetches[:5]:
        fetch.wait()
    live = (iota((1, faces), 1) < count_ref[0, 0]).astype(jnp.float32)
    load_s[...] = jnp.zeros_like(load_s)
    for a in range(trace_dim):
        load_s[a : a + 1, :] = load_ref[0, a] * live
    moved_s[...] = jnp.zeros_like(moved_s)

    def unpack(b, carry):
        for s in range(faces // LANES):
            for k in range(links + 1):
                couple_s[s, b, (k + 1) * rows - 8 : (k + 1) * rows, :] = jnp.zeros((8, LANES), jnp.float32)
        for a in range(trace_dim):
            blocks = couple_ref[0, 0, a, b].astype(jnp.float32)
            for s in range(faces // LANES):
                couple_s[s, b, pl.ds(a, links + 1, stride=rows), :] = blocks[:, s * LANES : (s + 1) * LANES]
        return carry

    coarse_send[...] = jnp.zeros_like(coarse_send)
    slots_s[...] = jnp.zeros_like(slots_s)
    inside = jnp.zeros((1, faces), jnp.float32)
    owner = jnp.full((1, faces), -1.0, jnp.float32)
    eye_slots = iota((cap, cap), 0) == iota((cap, cap), 1)
    face_ids = iota((cap, faces), 1).astype(jnp.float32)
    place = iota((cap, faces), 0)
    for j in range(peers):
        slot_row = slot_ref[0, 0, j : j + 1, :]
        slots_s[:, j * cap : (j + 1) * cap] = slot_row
        as_float = jnp.broadcast_to(slot_row.astype(jnp.float32), (cap, cap))
        column = jnp.sum(jnp.where(eye_slots, as_float, 0.0), axis=1, keepdims=True)
        hit = (column == face_ids) & (place < pair_ref[0, 0, j])
        found = jnp.max(jnp.where(hit, place.astype(jnp.float32), -1.0), axis=0, keepdims=True)
        inside = jnp.where(found >= 0.0, found, inside)
        owner = jnp.where(found >= 0.0, float(j), owner)
    interface_s[...] = jnp.where(owner >= 0.0, 1.0, 0.0)
    inside_s[...] = inside.astype(jnp.int32)
    owner_s[...] = owner.astype(jnp.int32)
    robin_s[...] = jnp.zeros_like(robin_s)
    trace_s[...] = omega_step * load_s[...]
    eye = iota((cvec, cvec), 0) == iota((cvec, cvec), 1)

    fetches[5].wait()
    lax.fori_loop(0, trace_dim, unpack, 0, unroll=3)
    count = (peers - 1) + jnp.where(g > 0, peers, 0) + jnp.where(g < groups - 1, peers, 0)

    def apply(x):
        stack_s[0] = x
        for k in range(links):
            stack_s[k + 1] = pick_lanes(x, link_ref[0, k])
        chunks = []
        for s in range(faces // LANES):
            lanes = slice(s * LANES, (s + 1) * LANES)
            totals = []
            for k in range(links + 1):
                total = None
                for b in range(trace_dim):
                    term = couple_s[s, b, k * rows : (k + 1) * rows, :] * stack_s[k, b : b + 1, lanes]
                    total = term if total is None else total + term
                totals.append(total)
            chunks.append(functools.reduce(jnp.add, totals))
        product = jnp.concatenate(chunks, axis=1)
        return live * (product + robin_weight * interface_s[...] * x)

    def right_side():
        return load_s[...] + live * robin_s[...]

    def sweep(x, bx):
        return x + omega_step * (right_side() - bx)

    def as_row(column):
        return jnp.sum(jnp.where(eye, column, 0.0), axis=0, keepdims=True)

    def send_row(t, r, row):
        coarse_send[t, r, :, 0:cvec] = row

        def push(d):
            for device in targets(d):
                pltpu.make_async_remote_copy(
                    src_ref=coarse_send.at[t, r],
                    dst_ref=coarse_recv.at[t, r, (1 - d) * peers + me],
                    send_sem=coarse_send_sem.at[t, r, 1 + d],
                    recv_sem=coarse_recv_sem.at[t, r, 1 - d],
                    device_id=device,
                    device_id_type=MESH,
                ).start()

        far_first(push)

    def wait_rows(t, r, sems):
        def wait(d):
            n = peers - 1 if d == 0 else peers
            part = coarse_recv.at[t, r, pl.ds((1 + d) * peers, n)]
            pltpu.make_async_copy(part, part, sems.at[t, r, 1 + d]).wait()

        per_group(wait)

    def coupled(t, r):
        table_s[...] = coarse_recv[t, r]
        total = None
        for k in range(kc):
            position = coarse_link_ref[0, 0, k] - (g - 1) * peers
            position = jnp.minimum(jnp.maximum(position, 0), 3 * peers - 1)
            term = folded_s[k] * table_s[position][:, 0:cvec]
            total = term if total is None else total + term
        return jnp.sum(total, axis=1, keepdims=True)

    def robin_copy(t, off):
        to = after(off)
        chunk = lax.div(to * cap, LANES)
        return pltpu.make_async_remote_copy(
            src_ref=robin_send.at[t, chunk],
            dst_ref=robin_recv.at[t, off - 1],
            send_sem=robin_send_sem.at[t, off - 1],
            recv_sem=robin_recv_sem.at[t, off - 1],
            device_id=(g, to),
            device_id_type=MESH,
        )

    def fold():
        for a in range(trace_dim):
            shared = pick_lanes(basis_ref[0, 0, a], slots_s[...])
            for s in range(slots_s.shape[1] // LANES):
                shared_s[s, a] = shared[:, s * LANES : (s + 1) * LANES]
        for k in range(kc):
            folded_s[k] = jnp.dot(
                inverse_ref[0, 0],
                block_ref[0, 0, k],
                precision=highest,
                preferred_element_type=jnp.float32,
            )

    def relax(bx):
        trace_s[...] = sweep(trace_s[...], bx)

    def prepare(t):
        outgoing = 2.0 * robin_weight * trace_s[...] - robin_s[...]
        sent = pick_lanes(outgoing, slots_s[...])
        for s in range(slots_s.shape[1] // LANES):
            robin_send[t, s] = sent[:, s * LANES : (s + 1) * LANES]

    def coarse(t, bx):
        residual = right_side() - bx
        part = jnp.zeros((cvec, LANES), jnp.float32)
        for a in range(trace_dim):
            product = basis_ref[0, 0, a] * residual[a : a + 1, :]
            for s in range(faces // LANES):
                part = part + product[:, s * LANES : (s + 1) * LANES]
        restricted = jnp.sum(part, axis=1, keepdims=True)
        start = jnp.sum(inverse_ref[0, 0] * as_row(restricted), axis=1, keepdims=True)
        coef = start
        for r in range(CSWEEPS):
            send_row(t, r, as_row(coef))
            if r == 0:
                pl.when(t == 0)(fold)
                prepare(t)
            wait_rows(t, r, coarse_recv_sem)
            coef = start - coupled(t, r)
        coef_s[...] = jnp.broadcast_to(coef, coef_s.shape)
        for s in range(slots_s.shape[1] // LANES):
            for a in range(trace_dim):
                moved = jnp.sum(shared_s[s, a] * coef_s[...], axis=0, keepdims=True)
                robin_send[t, s, a : a + 1, :] += 2.0 * robin_weight * moved
        for off in range(1, peers):
            robin_copy(t, off).start()
        coef_out[0] = as_row(coef)
        wide = jnp.concatenate([coef_s[...]] * (faces // LANES), axis=1)
        for a in range(trace_dim):
            moved_s[a : a + 1, :] = jnp.sum(basis_ref[0, 0, a] * wide, axis=0, keepdims=True)
        x = trace_s[...] + live * moved_s[...]
        trace_s[...] = x
        for a in range(trace_dim):
            trace_out[0, a] = x[a : a + 1, :]

    def settle(t, bx):
        base = lax.rem(me * cap, LANES)
        inside = inside_s[...] + base
        owner = owner_s[...]
        fresh = jnp.zeros((rows, faces), jnp.float32)
        for off in range(1, peers):
            robin_copy(t, off).wait_recv()
            source = after(peers - off)
            got = pick_lanes(robin_recv[t, off - 1], inside)
            fresh = jnp.where(owner == source, got, fresh)
        robin_s[...] = fresh
        trace_s[...] = sweep(trace_s[...], bx)
        for r in range(CSWEEPS):
            wait_rows(t, r, coarse_send_sem)
        for off in range(1, peers):
            robin_copy(t, off).wait_send()

    phases = SWEEPS + 1

    def step(n, carry):
        t = n // phases
        phase = n - t * phases
        bx = apply(trace_s[...])
        pl.when(phase < SWEEPS - 1)(lambda: relax(bx))

        @pl.when(n == SWEEPS - 1)
        def _():
            pl.semaphore_wait(barrier, count)
            for fetch in fetches[6:]:
                fetch.wait()

        pl.when(phase == SWEEPS - 1)(lambda: coarse(t, bx))
        pl.when(phase == SWEEPS)(lambda: settle(t, bx))
        return carry

    lax.fori_loop(0, ITERS * phases, step, 0)
    for a in range(trace_dim):
        robin_out[0, a] = robin_s[a : a + 1, :]


def solution(mesh):
    groups, peers = mesh.shape["grp"], mesh.shape["sub"]

    def body(
        load,
        couple,
        face_link,
        face_count,
        slot_face,
        pair_count,
        basis,
        coarse_inverse,
        coarse_block,
        coarse_link,
    ):
        trace_dim, faces = load.shape[-2:]
        rows = -(-trace_dim // 8) * 8
        links = face_link.shape[-2]
        cvec = basis.shape[2]
        kc = coarse_link.shape[-1]
        cap = slot_face.shape[-1]
        chunks = -(-peers * cap // LANES)
        vmem, smem = pltpu.VMEM, pltpu.SMEM
        operands = (
            jnp.swapaxes(load, 1, 2),
            jnp.transpose(couple, (0, 1, 3, 4, 2, 5)),
            jnp.swapaxes(face_link, 1, 2),
            face_count,
            slot_face,
            pair_count,
            jnp.swapaxes(basis, 2, 3),
            coarse_inverse,
            coarse_block,
            coarse_link,
        )
        f32 = jnp.float32
        spec = lambda space: pl.BlockSpec(memory_space=space)
        trace_field, robin_data, coefficients = pl.pallas_call(
            functools.partial(kernel, groups, peers),
            out_shape=(
                jax.ShapeDtypeStruct((1, trace_dim, 1, faces), f32),
                jax.ShapeDtypeStruct((1, trace_dim, 1, faces), f32),
                jax.ShapeDtypeStruct((1, 1, cvec), f32),
            ),
            in_specs=[spec(pl.ANY)] * len(operands),
            out_specs=(spec(vmem), spec(vmem), spec(vmem)),
            scratch_shapes=[
                space(x.shape, x.dtype)
                for x, space in zip(operands, (vmem, vmem, vmem, smem, vmem, smem, vmem, vmem, vmem, smem))
            ]
            + [
                vmem((rows, faces), f32),
                vmem((rows, faces), f32),
                vmem((rows, faces), f32),
                vmem((links + 1, rows, faces), f32),
                vmem((faces // LANES, trace_dim, (links + 1) * rows, LANES), f32),
                vmem((rows, faces), f32),
                vmem((3 * peers, 1, LANES), f32),
                vmem((kc, cvec, cvec), f32),
                vmem((chunks, trace_dim, cvec, LANES), f32),
                vmem((1, chunks * LANES), jnp.int32),
                vmem((1, faces), jnp.int32),
                vmem((1, faces), jnp.int32),
                vmem((1, faces), f32),
                vmem((cvec, LANES), f32),
                vmem((ITERS, CSWEEPS, 1, LANES), f32),
                vmem((ITERS, CSWEEPS, 3 * peers, 1, LANES), f32),
                vmem((ITERS, chunks, rows, LANES), f32),
                vmem((ITERS, peers - 1, rows, LANES), f32),
                pltpu.SemaphoreType.DMA((ITERS, CSWEEPS, 3)),
                pltpu.SemaphoreType.DMA((ITERS, CSWEEPS, 3)),
                pltpu.SemaphoreType.DMA((ITERS, peers - 1)),
                pltpu.SemaphoreType.DMA((ITERS, peers - 1)),
                pltpu.SemaphoreType.DMA((len(operands),)),
            ],
            compiler_params=pltpu.CompilerParams(
                collective_id=0, has_side_effects=True, vmem_limit_bytes=24 * 1024 * 1024
            ),
        )(*(x if x.size == 1 else pltpu.with_memory_space_constraint(x, pltpu.HBM) for x in operands))
        return jnp.swapaxes(trace_field, 1, 2), jnp.swapaxes(robin_data, 1, 2), coefficients

    in_specs = (
        P("grp", "sub", None, None),
        P("grp", "sub", None, None, None, None),
        P("grp", "sub", None, None),
        P("grp", "sub"),
        P("grp", "sub", None, None),
        P("grp", "sub", None),
        P("grp", "sub", None, None, None),
        P("grp", "sub", None, None),
        P("grp", "sub", None, None, None),
        P("grp", "sub", None),
    )
    out_specs = (P("grp", "sub", None, None), P("grp", "sub", None, None), P("grp", "sub", None))
    return jax.shard_map(body, mesh=mesh, in_specs=in_specs, out_specs=out_specs, check_vma=False)
```
